128 devices in a mesh: row: 8 (over y, core), col: 16 (over z, x).
Axes of the slice: x: 4, y: 4, z: 4, core: 2. Of those that a mesh axis runs over, the one named last changes fastest.
Arguments:
- state: float32 [2, 262144], P(None, ('row', 'col')), may hold values from -2.5 to 2.5
- friction: float32 [3, 262144], P(None, ('row', 'col')), as said below
- near_blocks: bfloat16 [1024, 256, 256], P(('row', 'col')), as said below
- left_factor: bfloat16 [16384, 64, 256], P(('row', 'col')), may hold values from -0.1875 to 0.1875
- right_factor: bfloat16 [16384, 64, 256], P(('row', 'col')), may hold values from -0.375 to 0.375
- pairs: int32 [16384, 2], P(('row', 'col')), may hold values from 0 to 1023, as said below
- ranks: int32 [16384], P(('row', 'col')), may hold values from 8 to 64, as said below
- perm: int32 [262144], P(('row', 'col')), may hold values from 0 to 262143, as said below
Outputs:
- new_state: float32 [2, 262144], P(None, ('row', 'col'))
- error_norm: float32 [], replicated
The draws below stay inside these ranges and needn't reach their ends.
Inputs may be any that keep to these rules, and one draw needn't show every extreme that they name: `pairs`: pairs are held in blocks of 128 rows, the block of device d = i * 16 + j on row+col. In that block the first cluster lies in i * 16 * 8 to (i + 1) * 16 * 8 - 1 and the second cluster is (k * 16 + j) * 8 + e with k != i and 0 <= e < 8. `ranks`: multiples of 8. `perm`: A permutation that maps each block of 2048 consecutive positions onto the same block. `friction`: all entries positive. `near_blocks`: each block is symmetric.
All inputs are finite; a program needn't handle non-finite values.
Results may differ from the reference program's by a relative error of at most 0.00055.
Values may be sent and summed in bfloat16 or wider, within the bound.
No kernel may reach another device: no remote copies, remote signals or barrier semaphores. Data moves between devices by JAX's collectives and lax.ppermute only.
A program may use at most 64 MiB of HBM per device.

```python
import jax
import jax.numpy as jnp
from jax import lax

CS = 256
RMAX = 64
CPD = 8
PD = 128
NC = 1024
PATCHES = 262144
NPAIRS = 16384
N_ROW = 8
N_COL = 16


def draw_friction(key, part):
    key = jax.random.fold_in(key, 1)
    key_a, key_b, key_s = jax.random.split(key, 3)
    coef_a = jnp.exp(jax.random.uniform(key_a, (PATCHES,), jnp.float32, jnp.log(0.3), jnp.log(1.0)))
    coef_b = jnp.exp(jax.random.uniform(key_b, (PATCHES,), jnp.float32, jnp.log(0.3), jnp.log(1.5)))
    rough = jnp.exp(jax.random.uniform(key_s, (PATCHES,), jnp.float32, jnp.log(0.7), jnp.log(1.4)))
    depth = jnp.arange(PATCHES, dtype=jnp.float32) / max(PATCHES - 1, 1)
    sigma = (1.0 + 2.0 * depth) * rough
    return jnp.stack([coef_a, coef_b, sigma]).astype(jnp.float32)


def draw_near_blocks(key, part):
    key = jax.random.fold_in(key, 2)
    key_o, key_d = jax.random.split(key)
    loose = jax.random.normal(key_o, (NC, CS, CS), jnp.float32)
    loose = loose / jnp.sqrt(float(CS))
    sym = 0.5 * (loose + jnp.swapaxes(loose, 1, 2))
    diag = 2.0 + jax.random.uniform(key_d, (NC, CS), jnp.float32)
    eye = (jnp.arange(CS)[:, None] == jnp.arange(CS)[None, :]).astype(jnp.float32)
    return (sym * (1.0 - eye) + eye * diag[:, :, None]).astype(jnp.bfloat16)


def draw_pairs(key, part):
    key = jax.random.fold_in(key, 3)
    key_a, key_b, key_c = jax.random.split(key, 3)
    slot = jnp.arange(NPAIRS, dtype=jnp.int32)
    device = slot // PD
    row_i = device // N_COL
    col_j = device % N_COL
    span = N_COL * CPD
    first = row_i * span + jax.random.randint(key_a, (NPAIRS,), 0, span)
    other = (row_i + 1 + jax.random.randint(key_b, (NPAIRS,), 0, N_ROW - 1)) % N_ROW
    second = (other * N_COL + col_j) * CPD + jax.random.randint(key_c, (NPAIRS,), 0, CPD)
    return jnp.stack([first, second], axis=1).astype(jnp.int32)


def draw_ranks(key, part):
    key = jax.random.fold_in(key, 4)
    key_t, key_r = jax.random.split(key)
    steps = RMAX // 8
    top = jax.random.randint(key_t, (NPAIRS // PD,), 1, steps + 1)
    slot = jnp.arange(NPAIRS, dtype=jnp.int32)
    top_slot = top[slot // PD]
    level = jax.random.randint(key_r, (NPAIRS,), 0, steps) % top_slot
    ranks = 8 * (1 + level)
    return jnp.where(slot % PD == 0, RMAX, ranks).astype(jnp.int32)


def draw_perm(key, part):
    key = jax.random.fold_in(key, 5)
    blocks = NC // CPD
    keys = jax.random.split(key, blocks)
    local = jax.vmap(lambda k: jax.random.permutation(k, CPD * CS))(keys)
    offsets = jnp.arange(blocks, dtype=jnp.int32)[:, None] * (CPD * CS)
    return (local.astype(jnp.int32) + offsets).reshape(-1).astype(jnp.int32)


def block_scale(key, dims, pieces, smallest, high):
    gain, own = 1.0, jax.random.fold_in(key, 6)
    for position, parts in pieces:
        steps = jnp.exp(jax.random.uniform(jax.random.fold_in(own, position), (parts,), jnp.float32, smallest / len(pieces), high / len(pieces)))
        gain = gain * jnp.repeat(steps, dims[position] // parts).reshape([-1 if axis == position else 1 for axis in range(len(dims))])
    return gain


def normal_values(stream_key, extent, width, reach, pieces=(), kind=jnp.bfloat16):
    entries = width * jax.random.normal(stream_key, extent, jnp.float32)
    if pieces:
        entries = entries * block_scale(stream_key, extent, pieces, -0.22, 0.18)
    return jnp.clip(entries, -reach, reach).astype(kind)


def setup_inputs(seed: int = 0) -> dict:
    arg_keys = jax.random.split(jax.random.key(seed), 9)
    return {
        "state": normal_values(arg_keys[0], (2, PATCHES), 0.4, 2.5, ((1, 128),), jnp.float32),
        "friction": draw_friction(jax.random.fold_in(arg_keys[8], 71), 0),
        "near_blocks": draw_near_blocks(jax.random.fold_in(arg_keys[8], 71), 0),
        "left_factor": normal_values(arg_keys[3], (NPAIRS, RMAX, CS), (RMAX * PD // CPD) ** -0.5, 0.1875, ((0, 128),)),
        "right_factor": normal_values(arg_keys[4], (NPAIRS, RMAX, CS), CS ** -0.5, 0.375, ((0, 128),)),
        "pairs": draw_pairs(jax.random.fold_in(arg_keys[8], 71), 0),
        "ranks": draw_ranks(jax.random.fold_in(arg_keys[8], 71), 0),
        "perm": draw_perm(jax.random.fold_in(arg_keys[8], 71), 0),
    }


step_size = 0.1
damping = 0.5
abs_tol = 0.001
rel_tol = 0.001

def round_half(value):
    return lax.optimization_barrier(value.astype(jnp.bfloat16)).astype(jnp.float32)

def cluster_stress(ordered, near_blocks, left_factor, right_factor, pairs, ranks):
    ordered_f = ordered.astype(jnp.float32)
    total = jnp.einsum('qij,qj->qi', near_blocks.astype(jnp.float32), ordered_f)
    blocks = NPAIRS // PD
    xs = (left_factor.reshape(blocks, PD, RMAX, CS), right_factor.reshape(blocks, PD, RMAX, CS), pairs.reshape(blocks, PD, 2), ranks.reshape(blocks, PD))

    def add_block(acc, piece):
        left_b, right_b, pair_b, rank_b = piece
        mask = (jnp.arange(RMAX, dtype=jnp.int32)[None, :] < rank_b[:, None]).astype(jnp.float32)
        left_f = left_b.astype(jnp.float32)
        right_f = right_b.astype(jnp.float32)
        first = ordered_f[pair_b[:, 0]]
        second = ordered_f[pair_b[:, 1]]
        coef_j = round_half(jnp.einsum('prc,pc->pr', right_f, second) * mask)
        coef_i = round_half(jnp.einsum('prc,pc->pr', left_f, first) * mask)
        to_first = jnp.einsum('prc,pr->pc', left_f, coef_j)
        to_second = jnp.einsum('prc,pr->pc', right_f, coef_i)
        acc = acc.at[pair_b[:, 0]].add(to_first).at[pair_b[:, 1]].add(to_second)
        return (acc, None)
    total, _ = lax.scan(add_block, total, xs)
    return total

def derivative(current, friction, near_blocks, left_factor, right_factor, pairs, ranks, perm):
    rate = jnp.exp(current[0])
    deficit = (1.0 - rate).astype(jnp.bfloat16)
    ordered = deficit[perm].reshape(NC, CS)
    stress = cluster_stress(ordered, near_blocks, left_factor, right_factor, pairs, ranks)
    stress_rate = jnp.zeros((PATCHES,), jnp.float32).at[perm].set(stress.reshape(-1))
    coef_a, coef_b, sigma = (friction[0], friction[1], friction[2])
    dlt = jnp.exp(-current[1]) - rate
    dlv = (stress_rate - coef_b * sigma * dlt) / (coef_a * sigma + damping * rate)
    return jnp.stack([dlv, dlt])

def reference(state, friction, near_blocks, left_factor, right_factor, pairs, ranks, perm):
    first_k = derivative(state, friction, near_blocks, left_factor, right_factor, pairs, ranks, perm)
    section = state + step_size * first_k
    second_k = derivative(section, friction, near_blocks, left_factor, right_factor, pairs, ranks, perm)
    new_state = state + 0.5 * step_size * (first_k + second_k)
    scaled = 0.5 * step_size * (second_k - first_k) / (abs_tol + rel_tol * jnp.abs(new_state))
    error_norm = jnp.sqrt(jnp.sum(scaled * scaled) / (2.0 * PATCHES))
    return (new_state, error_norm)
```

```python
import functools

import jax
import jax.numpy as jnp
from jax import lax
from jax.experimental import pallas as pl
from jax.experimental.pallas import tpu as pltpu
from jax.sharding import PartitionSpec as P

step_size = 0.1
damping = 0.5
abs_tol = 0.001
rel_tol = 0.001

f32 = jnp.float32
bf16 = jnp.bfloat16
LANES = 128
VMEM = pl.BlockSpec(memory_space=pltpu.VMEM)
HBM = pl.BlockSpec(memory_space=pl.ANY)


def mxu(a, b):
    return lax.dot_general(a, b, (((1,), (0,)), ((), ())), preferred_element_type=f32)


def mxu_nt(a, b):
    return lax.dot_general(a, b, (((1,), (1,)), ((), ())), preferred_element_type=f32)


def to_tiles(row):
    return jnp.concatenate([row[:, k * LANES:(k + 1) * LANES] for k in range(row.shape[1] // LANES)], axis=0)


def to_row(tiles):
    return jnp.concatenate([tiles[k:k + 1, :] for k in range(tiles.shape[0])], axis=1)


def to_clusters(row, cluster):
    return jnp.concatenate([row[:, k * cluster:(k + 1) * cluster] for k in range(row.shape[1] // cluster)], axis=0)


def split3(x):
    hi = x.astype(bf16)
    rest = x - hi.astype(f32)
    mid = rest.astype(bf16)
    low = (rest - mid.astype(f32)).astype(bf16)
    return hi, mid, low


def place(perm_row, tiles):
    count = perm_row.shape[1]
    local = lax.rem(perm_row, count)
    tile = lax.div(local, LANES)
    lane = local - tile * LANES
    at_tile = lax.broadcasted_iota(jnp.int32, (tiles, count), 0) == tile
    at_lane = lax.broadcasted_iota(jnp.int32, (LANES, count), 0) == lane
    return at_tile, jnp.where(at_lane, 1.0, 0.0).astype(bf16)


def spread(ordered, out_ref, copies):
    value = ordered.astype(bf16)
    for k in range(copies):
        out_ref[k] = value


def first_deficit(copies, state_ref, perm_ref, own_ref, copies_ref):
    cluster = own_ref.shape[1]
    at_tile, at_lane = place(perm_ref[...], perm_ref.shape[1] // LANES)
    deficit = to_tiles(1.0 - jnp.exp(state_ref[0:1, :])).astype(bf16)
    picked = jnp.where(at_tile, mxu(deficit, at_lane), 0.0)
    ordered = to_clusters(jnp.sum(picked, axis=0, keepdims=True), cluster)
    own_ref[...] = ordered
    spread(ordered, copies_ref, copies)


def to_order(state_ref, friction_ref, perm_ref, fields_ref):
    cluster = fields_ref.shape[2]
    tiles = perm_ref.shape[1] // LANES
    at_tile, at_lane = place(perm_ref[...], tiles)
    coef_a, coef_b, sigma = (friction_ref[k:k + 1, :] for k in range(3))
    rows = (state_ref[0:1, :], state_ref[1:2, :], coef_a * sigma, coef_b * sigma)
    parts = [part for row in rows for part in split3(to_tiles(row))]
    moved = mxu(jnp.concatenate(parts, axis=0), at_lane)
    for k in range(len(rows)):
        three = [moved[(3 * k + s) * tiles:(3 * k + s + 1) * tiles] for s in range(3)]
        picked = jnp.where(at_tile, (three[0] + three[1]) + three[2], 0.0)
        fields_ref[k] = to_clusters(jnp.sum(picked, axis=0, keepdims=True), cluster)


def from_order(new_ref, perm_ref, out_ref):
    tiles = perm_ref.shape[1] // LANES
    at_tile, at_lane = place(perm_ref[...], tiles)
    parts = []
    for k in range(2):
        row = to_row_of_clusters(new_ref[k])
        parts += [jnp.where(at_tile, part.astype(f32), 0.0).astype(bf16) for part in split3(row)]
    moved = mxu_nt(jnp.concatenate(parts, axis=0), at_lane)
    for k in range(2):
        three = [moved[(3 * k + s) * tiles:(3 * k + s + 1) * tiles] for s in range(3)]
        out_ref[k:k + 1, :] = to_row((three[0] + three[1]) + three[2])


def to_row_of_clusters(x):
    return jnp.concatenate([x[k:k + 1, :] for k in range(x.shape[0])], axis=1)


def stress_terms(chunk, everyone_ref, own_ref, partner_ref, y1_ref, y2_ref, y3_ref, sel_ref, near_hbm, left_hbm,
                 right_hbm, first_ref, *rest):
    second_refs = rest[:4]
    near, left, right, sem = rest[4:]
    total = left.shape[0]
    chunks = total // chunk

    def fetch(k):
        part = pl.ds(k * chunk, chunk)
        return (
            pltpu.make_async_copy(right_hbm.at[part], right.at[part], sem.at[0, k]),
            pltpu.make_async_copy(left_hbm.at[part], left.at[part], sem.at[1, k]),
        )

    near_copy = pltpu.make_async_copy(near_hbm, near, sem.at[0, chunks])
    for k in range(chunks):
        for copy in fetch(k):
            copy.start()
    near_copy.start()

    everyone = everyone_ref[...]
    own = own_ref[...]
    group = jnp.concatenate([own, partner_ref[...], y1_ref[...], y2_ref[...], y3_ref[...]], axis=0).astype(bf16)
    firsts, seconds = everyone.shape[0], group.shape[0]
    row_first = lax.broadcasted_iota(jnp.int32, (firsts, chunk), 0)
    row_second = lax.broadcasted_iota(jnp.int32, (seconds, chunk), 0)
    to_first = jnp.zeros((firsts, own.shape[1]), f32)
    to_second = jnp.zeros((seconds, own.shape[1]), f32)
    for k in range(chunks):
        part = pl.ds(k * chunk, chunk)
        at_first = row_first == sel_ref[0:1, part]
        at_second = row_second == sel_ref[1:2, part]
        copy_right, copy_left = fetch(k)
        copy_right.wait()
        r = right[part]
        coef_j = jnp.sum(jnp.where(at_second, mxu_nt(group, r), 0.0), axis=0, keepdims=True)
        copy_left.wait()
        l = left[part]
        coef_i = jnp.sum(jnp.where(at_first, mxu_nt(everyone, l), 0.0), axis=0, keepdims=True)
        to_first += mxu(jnp.where(at_first, coef_j, 0.0).astype(bf16), l)
        to_second += mxu(jnp.where(at_second, coef_i, 0.0).astype(bf16), r)
    near_copy.wait()
    mine = own.astype(bf16)
    count = own.shape[0]
    row_own = lax.broadcasted_iota(jnp.int32, own.shape, 0)
    near_term = jnp.zeros(own.shape, f32)
    for k in range(count):
        near_term += jnp.where(row_own == k, mxu(mine, near[k]), 0.0)
    first_ref[...] = to_first.astype(first_ref.dtype)
    for k, ref in enumerate(second_refs):
        ref[...] = to_second[2 * count * k:2 * count * (k + 1)]
    second_refs[0][0:count, :] += near_term


def slopes(lv, lt, a_sigma, b_sigma, stress):
    rate = jnp.exp(lv)
    dlt = jnp.exp(-lt) - rate
    return (stress - b_sigma * dlt) / (a_sigma + damping * rate), dlt


def total_stress(from_first_ref, kept_ref, partner_ref):
    total = kept_ref[...] + partner_ref[...]
    for k in range(from_first_ref.shape[0]):
        total += from_first_ref[k].astype(f32)
    return total


def half_step(copies, from_first_ref, kept_ref, partner_ref, fields_ref, slope_ref, own_ref, copies_ref):
    lv, lt, a_sigma, b_sigma = (fields_ref[k] for k in range(4))
    dlv, dlt = slopes(lv, lt, a_sigma, b_sigma, total_stress(from_first_ref, kept_ref, partner_ref))
    slope_ref[0] = dlv
    slope_ref[1] = dlt
    ordered = (1.0 - jnp.exp(lv + step_size * dlv)).astype(bf16).astype(f32)
    own_ref[...] = ordered
    spread(ordered, copies_ref, copies)


def last_step(from_first_ref, kept_ref, partner_ref, fields_ref, slope_ref, new_ref, sum_ref):
    lv, lt, a_sigma, b_sigma = (fields_ref[k] for k in range(4))
    stress = total_stress(from_first_ref, kept_ref, partner_ref)
    first = (slope_ref[0], slope_ref[1])
    second = slopes(lv + step_size * first[0], lt + step_size * first[1], a_sigma, b_sigma, stress)
    squares = jnp.zeros(lv.shape, f32)
    for k, base in enumerate((lv, lt)):
        new = base + 0.5 * step_size * (first[k] + second[k])
        new_ref[k] = new
        scaled = 0.5 * step_size * (second[k] - first[k]) / (abs_tol + rel_tol * jnp.abs(new))
        squares += scaled * scaled
    sum_ref[...] = jnp.full(sum_ref.shape, jnp.sum(squares), f32)


def call(kernel, out_shape, ins, name, scratch=()):
    many = isinstance(out_shape, (list, tuple))
    return pl.pallas_call(
        kernel,
        out_shape=out_shape,
        in_specs=ins,
        out_specs=[VMEM] * len(out_shape) if many else VMEM,
        scratch_shapes=list(scratch),
        name=name,
        compiler_params=pltpu.CompilerParams(vmem_limit_bytes=32 * 1024 * 1024),
    )


def shards(rows, columns, state, friction, near_blocks, left_factor, right_factor, pairs, ranks, perm):
    own_count, cluster = near_blocks.shape[:2]
    count, width = left_factor.shape[:2]
    span = columns * own_count
    sds = jax.ShapeDtypeStruct
    block = sds((own_count, cluster), f32)
    copies = sds((columns, own_count, cluster), bf16)
    row = lax.axis_index("row")
    perm_row = perm.reshape(1, -1)

    def swap(x, distance):
        return lax.ppermute(x, "row", [(r, r ^ distance) for r in range(rows)])

    own, spread_out = call(functools.partial(first_deficit, columns), [block, copies], [VMEM] * 2, "first_deficit")(
        state, perm_row)
    fields = call(to_order, sds((4, own_count, cluster), f32), [VMEM] * 3, "to_order")(state, friction, perm_row)

    first_at = pairs[:, 0] - row * span
    second_at = ((pairs[:, 1] // span) ^ row) * own_count + pairs[:, 1] % own_count
    within = jnp.arange(width, dtype=jnp.int32)[None, :] < ranks[:, None]
    sel = jnp.stack([
        jnp.where(within, first_at[:, None], -1).reshape(-1),
        jnp.where(within, second_at[:, None], -1).reshape(-1),
    ])
    left = left_factor.reshape(count * width, cluster)
    right = right_factor.reshape(count * width, cluster)

    chunk = 2048
    pair_block = sds((2 * own_count, cluster), f32)
    terms = call(
        functools.partial(stress_terms, chunk),
        [sds((span, cluster), bf16)] + [pair_block] * 4,
        [VMEM] * 7 + [HBM] * 3,
        "stress_terms",
        [
            pltpu.VMEM(near_blocks.shape, bf16),
            pltpu.VMEM(left.shape, bf16),
            pltpu.VMEM(right.shape, bf16),
            pltpu.SemaphoreType.DMA((2, count * width // chunk + 1)),
        ],
    )

    def exchange(own, spread_out):
        everyone = lax.all_to_all(spread_out, "col", 0, 0)
        partner = swap(own, 1)
        two = jnp.concatenate([own, partner], axis=0)
        others = [swap(two, 2 * k) for k in (1, 2, 3)]
        first, *second = terms(everyone.reshape(span, cluster), own, partner, *others, sel, near_blocks, left, right)
        from_first = lax.all_to_all(first.reshape(columns, own_count, cluster), "col", 0, 0)
        both = second[0] + swap(second[1], 2) + swap(second[2], 4) + swap(second[3], 6)
        return from_first, both[:own_count], swap(both[own_count:], 1)

    slope, own, spread_out = call(
        functools.partial(half_step, columns), [sds((2, own_count, cluster), f32), block, copies], [VMEM] * 4, "half_step"
    )(*exchange(own, spread_out), fields)
    devices = rows * columns
    new, squares = call(
        last_step, [sds((2, own_count, cluster), f32), sds((devices, LANES), f32)], [VMEM] * 5, "last_step"
    )(*exchange(own, spread_out), fields, slope)
    everywhere = lax.all_to_all(squares, ("row", "col"), 0, 0, tiled=True)
    new_state = call(from_order, sds(state.shape, f32), [VMEM] * 2, "from_order")(new, perm_row)
    entries = 2.0 * state.shape[1] * devices
    return new_state, jnp.sqrt(jnp.sum(everywhere[:, 0]) / entries)


def solution(mesh):
    both = ("row", "col")
    placed = (P(None, both), P(None, both), P(both, None, None), P(both, None, None), P(both, None, None),
              P(both, None), P(both), P(both))
    return jax.shard_map(
        functools.partial(shards, mesh.shape["row"], mesh.shape["col"]),
        mesh=mesh,
        in_specs=placed,
        out_specs=(P(None, both), P()),
        check_vma=False,
    )
```

```python
import functools

import jax
import jax.numpy as jnp
from jax import lax
from jax.experimental import pallas as pl
from jax.experimental.pallas import tpu as pltpu
from jax.sharding import PartitionSpec as P

step_size = 0.1
damping = 0.5
abs_tol = 0.001
rel_tol = 0.001

f32 = jnp.float32
bf16 = jnp.bfloat16
LANES = 128
PAIRS = 16
VMEM = pl.BlockSpec(memory_space=pltpu.VMEM)


def mxu(a, b):
    return lax.dot_general(a, b, (((1,), (0,)), ((), ())), preferred_element_type=f32)


def mxu_nt(a, b):
    return lax.dot_general(a, b, (((1,), (1,)), ((), ())), preferred_element_type=f32)


def to_tiles(row):
    return jnp.concatenate([row[:, k * LANES:(k + 1) * LANES] for k in range(row.shape[1] // LANES)], axis=0)


def to_row(tiles):
    return jnp.concatenate([tiles[k:k + 1, :] for k in range(tiles.shape[0])], axis=1)


def to_clusters(row, cluster):
    return jnp.concatenate([row[:, k * cluster:(k + 1) * cluster] for k in range(row.shape[1] // cluster)], axis=0)


def split3(x):
    hi = x.astype(bf16)
    rest = x - hi.astype(f32)
    mid = rest.astype(bf16)
    low = (rest - mid.astype(f32)).astype(bf16)
    return hi, mid, low


def place(perm_row, tiles):
    count = perm_row.shape[1]
    local = lax.rem(perm_row, count)
    tile = lax.div(local, LANES)
    lane = local - tile * LANES
    at_tile = lax.broadcasted_iota(jnp.int32, (tiles, count), 0) == tile
    at_lane = lax.broadcasted_iota(jnp.int32, (LANES, count), 0) == lane
    return at_tile, jnp.where(at_lane, 1.0, 0.0).astype(bf16)


def first_deficit(state_ref, perm_ref, own_ref):
    cluster = own_ref.shape[1]
    at_tile, at_lane = place(perm_ref[...], perm_ref.shape[1] // LANES)
    deficit = to_tiles(1.0 - jnp.exp(state_ref[0:1, :])).astype(bf16)
    picked = jnp.where(at_tile, mxu(deficit, at_lane), 0.0)
    own_ref[...] = to_clusters(jnp.sum(picked, axis=0, keepdims=True), cluster)


def to_order(state_ref, friction_ref, perm_ref, fields_ref):
    cluster = fields_ref.shape[2]
    tiles = perm_ref.shape[1] // LANES
    at_tile, at_lane = place(perm_ref[...], tiles)
    coef_a, coef_b, sigma = (friction_ref[k:k + 1, :] for k in range(3))
    rows = (state_ref[0:1, :], state_ref[1:2, :], coef_a * sigma, coef_b * sigma)
    parts = [part for row in rows for part in split3(to_tiles(row))]
    moved = mxu(jnp.concatenate(parts, axis=0), at_lane)
    for k in range(len(rows)):
        three = [moved[(3 * k + s) * tiles:(3 * k + s + 1) * tiles] for s in range(3)]
        picked = jnp.where(at_tile, (three[0] + three[1]) + three[2], 0.0)
        fields_ref[k] = to_clusters(jnp.sum(picked, axis=0, keepdims=True), cluster)


def from_order(new_ref, perm_ref, out_ref):
    tiles = perm_ref.shape[1] // LANES
    at_tile, at_lane = place(perm_ref[...], tiles)
    parts = []
    for k in range(2):
        row = to_row_of_clusters(new_ref[k])
        parts += [jnp.where(at_tile, part.astype(f32), 0.0).astype(bf16) for part in split3(row)]
    moved = mxu_nt(jnp.concatenate(parts, axis=0), at_lane)
    for k in range(2):
        three = [moved[(3 * k + s) * tiles:(3 * k + s + 1) * tiles] for s in range(3)]
        out_ref[k:k + 1, :] = to_row((three[0] + three[1]) + three[2])


def to_row_of_clusters(x):
    return jnp.concatenate([x[k:k + 1, :] for k in range(x.shape[0])], axis=1)


def one_hot(mask):
    return jnp.where(mask, 1.0, 0.0).astype(bf16)


def collect(mask, terms):
    hot = one_hot(mask)
    high, mid, low = split3(terms)
    return mxu(hot, high) + (mxu(hot, mid) + mxu(hot, low))


def picked(at, values):
    hot = one_hot(lax.broadcasted_iota(jnp.int32, (at.shape[0], values.shape[0]), 1) == at)
    return mxu(hot, values).astype(bf16)


def stress_terms(chunk, everyone_ref, line_ref, more_ref, info_ref, col_ref, left_hbm, right_hbm, first_ref, kept_ref,
                 sent_ref, left, right, sem):
    pairs = info_ref.shape[1]
    width = left.shape[0] // pairs
    chunks = left.shape[0] // chunk

    def fetch(k):
        part = pl.ds(k * chunk, chunk)
        return (
            pltpu.make_async_copy(right_hbm.at[part], right.at[part], sem.at[0, k]),
            pltpu.make_async_copy(left_hbm.at[part], left.at[part], sem.at[1, k]),
        )

    for k in range(chunks):
        for copy in fetch(k):
            copy.start()
    line = jnp.concatenate([line_ref[...], more_ref[...]], axis=0).astype(bf16)
    x_first = picked(col_ref[:, 0:1], everyone_ref[...])
    x_second = picked(col_ref[:, 1:2], line)
    shape = (PAIRS, PAIRS * width)
    rank = lax.broadcasted_iota(jnp.int32, shape, 1) - width * lax.broadcasted_iota(jnp.int32, shape, 0)
    to_first, to_second = [], []
    for k in range(pairs // PAIRS):
        if k * shape[1] % chunk == 0:
            for copy in fetch(k * shape[1] // chunk):
                copy.wait()
        rows = slice(k * PAIRS, (k + 1) * PAIRS)
        part = pl.ds(k * shape[1], shape[1])
        within = (rank >= 0) & (rank < col_ref[rows, 2:3])
        coef_j = jnp.where(within, mxu_nt(x_second[rows], right[part]), 0.0).astype(bf16)
        coef_i = jnp.where(within, mxu_nt(x_first[rows], left[part]), 0.0).astype(bf16)
        to_first.append(mxu(coef_j, left[part]))
        to_second.append(mxu(coef_i, right[part]))
    first_ref[...] = sums_at(info_ref, 0, first_ref.shape[0], jnp.concatenate(to_first, axis=0)).astype(bf16)
    halves(sums_at(info_ref, 1, 2 * kept_ref.shape[0], jnp.concatenate(to_second, axis=0)), kept_ref, sent_ref)


def sums_at(info_ref, side, rows, terms):
    at = lax.broadcasted_iota(jnp.int32, (rows, info_ref.shape[1]), 0) == info_ref[side:side + 1, :]
    return collect(at, terms)


def halves(x, kept_ref, sent_ref):
    step = kept_ref.shape[0]
    kept_ref[...] = x[:step]
    sent_ref[...] = x[step:].astype(sent_ref.dtype)


def join(held_ref, received_ref, out_ref):
    out_ref[...] = jnp.concatenate([held_ref[...], received_ref[...]], axis=0)


def join_and_spread(held_ref, received_ref, out_ref, copies_ref):
    join(held_ref, received_ref, out_ref)
    for k in range(copies_ref.shape[0]):
        copies_ref[k] = held_ref[...].astype(bf16)


def add(held_ref, received_ref, *out_refs):
    halves(held_ref[...] + received_ref[...], *out_refs)


def place_of(difference):
    return difference ^ ((difference >> 1) & 1)


def pair_info(own_count, columns, pairs_ref, ranks_ref, info_ref, col_ref):
    row = lax.axis_index("row")
    owner = lax.div(pairs_ref[...], own_count)
    inside = pairs_ref[...] - owner * own_count
    owner_row = lax.div(owner, columns)
    by_row = owner_row ^ row
    first_at = (owner - owner_row * columns) * own_count + inside
    second_at = ((by_row & 1) + 2 * place_of(by_row >> 1)) * own_count + inside
    count = ranks_ref.shape[1]
    sublane = lax.broadcasted_iota(jnp.int32, (count, LANES), 0)
    lane = lax.broadcasted_iota(jnp.int32, (count, LANES), 1)
    rank = jnp.sum(jnp.where(sublane == lane, jnp.broadcast_to(ranks_ref[...], (count, LANES)), 0), axis=1, keepdims=True)
    columns_of = jnp.where(lane == 0, first_at[:, 0:1], jnp.where(lane == 1, second_at[:, 1:2], rank))
    col_ref[...] = columns_of
    info_ref[...] = jnp.transpose(columns_of)[:info_ref.shape[0]]


def near_terms(own_ref, near, out_ref):
    own = own_ref[...]
    row_own = lax.broadcasted_iota(jnp.int32, own.shape, 0)
    mine = own.astype(bf16)
    total = jnp.zeros(own.shape, f32)
    for k in range(own.shape[0]):
        total += jnp.where(row_own == k, mxu(mine, near[k]), 0.0)
    out_ref[...] = total


def slopes(lv, lt, a_sigma, b_sigma, stress):
    rate = jnp.exp(lv)
    dlt = jnp.exp(-lt) - rate
    return (stress - b_sigma * dlt) / (a_sigma + damping * rate), dlt


def total_stress(refs):
    near_ref, from_first_ref, kept_ref, received_ref = refs
    parts = [from_first_ref[k].astype(f32) for k in range(from_first_ref.shape[0])]
    while len(parts) > 1:
        parts = [parts[k] + parts[k + 1] for k in range(0, len(parts), 2)]
    return (near_ref[...] + parts[0]) + (kept_ref[...] + received_ref[...])


def half_step(*refs):
    *stress_refs, fields_ref, slope_ref, own_ref = refs
    lv, lt, a_sigma, b_sigma = (fields_ref[k] for k in range(4))
    dlv, dlt = slopes(lv, lt, a_sigma, b_sigma, total_stress(stress_refs))
    slope_ref[0] = dlv
    slope_ref[1] = dlt
    own_ref[...] = (1.0 - jnp.exp(lv + step_size * dlv)).astype(bf16).astype(f32)


def last_step(*refs):
    *stress_refs, fields_ref, slope_ref, new_ref, sum_ref = refs
    lv, lt, a_sigma, b_sigma = (fields_ref[k] for k in range(4))
    first = (slope_ref[0], slope_ref[1])
    second = slopes(lv + step_size * first[0], lt + step_size * first[1], a_sigma, b_sigma, total_stress(stress_refs))
    squares = jnp.zeros(lv.shape, f32)
    for k, base in enumerate((lv, lt)):
        new = base + 0.5 * step_size * (first[k] + second[k])
        new_ref[k] = new
        scaled = 0.5 * step_size * (second[k] - first[k]) / (abs_tol + rel_tol * jnp.abs(new))
        squares += scaled * scaled
    sum_ref[...] = jnp.full(sum_ref.shape, jnp.sum(squares), f32)


def in_hbm(x):
    return pltpu.with_memory_space_constraint(x, pltpu.HBM)


def call(kernel, out_shape, inputs, micros, scratch=(), streamed=()):
    many = isinstance(out_shape, (list, tuple))
    name = getattr(kernel, "func", kernel).__name__
    return pl.pallas_call(
        kernel,
        out_shape=out_shape,
        in_specs=[pl.BlockSpec(memory_space=pl.ANY) if any(x is y for y in streamed) else VMEM for x in inputs],
        out_specs=[VMEM] * len(out_shape) if many else VMEM,
        name=name,
        scratch_shapes=list(scratch),
        cost_estimate=pl.CostEstimate(flops=int(micros * 1.1e9), bytes_accessed=0, transcendentals=0),
        compiler_params=pltpu.CompilerParams(vmem_limit_bytes=32 * 1024 * 1024),
    )(*inputs)


def shards(rows, columns, state, friction, near_blocks, left_factor, right_factor, pairs, ranks, perm):
    own_count, cluster = near_blocks.shape[:2]
    count, width = left_factor.shape[:2]
    span = columns * own_count
    sds = jax.ShapeDtypeStruct
    block = sds((own_count, cluster), f32)
    perm_row = perm.reshape(1, -1)

    def swap(x, axis, distance):
        size = rows if axis == "row" else columns
        return lax.ppermute(x, axis, [(r, r ^ distance) for r in range(size)])

    own = call(first_deficit, block, [in_hbm(state), in_hbm(perm_row)], 6)
    fields = call(to_order, sds((4, own_count, cluster), f32), [state, friction, perm_row], 0.5)

    info, info_col = call(
        functools.partial(pair_info, own_count, columns),
        [sds((8, count), jnp.int32), sds((count, LANES), jnp.int32)], [pairs, ranks.reshape(1, -1)], 0.5)
    near = near_blocks
    left = in_hbm(left_factor.reshape(count * width, cluster))
    right = in_hbm(right_factor.reshape(count * width, cluster))

    def block_of(blocks, dtype):
        return sds((blocks * own_count, cluster), dtype)

    chunk = 2048
    scratch = [pltpu.VMEM(left.shape, bf16), pltpu.VMEM(right.shape, bf16),
               pltpu.SemaphoreType.DMA((2, count * width // chunk))]

    def exchange(own):
        two, copies = call(join_and_spread, [block_of(2, f32), sds((columns, own_count, cluster), bf16)],
                           [own, swap(own, "row", 1)], 0.2)
        four = call(join, block_of(4, f32), [two, swap(two, "row", 2)], 0.2)
        more = swap(four, "row", 6)
        everyone = lax.all_to_all(copies, "col", 0, 0).reshape(span, cluster)
        near_term = call(near_terms, block, [own, near], 0.3)
        first, kept, sent = call(
            functools.partial(stress_terms, chunk), [block_of(columns, bf16)] + [block_of(4, f32)] * 2,
            [everyone, four, more, info, info_col, left, right], 6, scratch, (left, right))
        for blocks, hop in ((2, 6), (1, 2)):
            kept, sent = call(add, [block_of(blocks, f32)] * 2, [kept, swap(sent, "row", hop)], 0.2)
        from_first = lax.all_to_all(first.reshape(columns, own_count, cluster), "col", 0, 0)
        return [near_term, from_first, kept, swap(sent, "row", 1)]

    slope, own = call(half_step, [sds((2, own_count, cluster), f32), block], [*exchange(own), fields], 0.1)
    devices = rows * columns
    new, squares = call(last_step, [sds((2, own_count, cluster), f32), sds((devices, LANES), f32)],
                        [*exchange(own), fields, slope], 0.8)
    everywhere = lax.all_to_all(squares, ("row", "col"), 0, 0, tiled=True)
    new_state = call(from_order, sds(state.shape, f32), [new, perm_row], 0.9)
    entries = 2.0 * state.shape[1] * devices
    return new_state, jnp.sqrt(jnp.sum(everywhere[:, 0]) / entries)


def solution(mesh):
    both = ("row", "col")
    placed = (P(None, both), P(None, both), P(both, None, None), P(both, None, None), P(both, None, None),
              P(both, None), P(both), P(both))
    return jax.shard_map(
        functools.partial(shards, mesh.shape["row"], mesh.shape["col"]),
        mesh=mesh,
        in_specs=placed,
        out_specs=(P(None, both), P()),
        check_vma=False,
    )
```

```python
import functools

import jax
import jax.numpy as jnp
from jax import lax
from jax.experimental import pallas as pl
from jax.experimental.pallas import tpu as pltpu
from jax.sharding import PartitionSpec as P

step_size = 0.1
damping = 0.5
abs_tol = 0.001
rel_tol = 0.001

f32 = jnp.float32
bf16 = jnp.bfloat16
LANES = 128
PAIRS = 16
VMEM = pl.BlockSpec(memory_space=pltpu.VMEM)


def mxu(a, b):
    return lax.dot_general(a, b, (((1,), (0,)), ((), ())), preferred_element_type=f32)


def mxu_nt(a, b):
    return lax.dot_general(a, b, (((1,), (1,)), ((), ())), preferred_element_type=f32)


def to_tiles(row):
    return jnp.concatenate([row[:, k * LANES:(k + 1) * LANES] for k in range(row.shape[1] // LANES)], axis=0)


def to_row(tiles):
    return jnp.concatenate([tiles[k:k + 1, :] for k in range(tiles.shape[0])], axis=1)


def to_clusters(row, cluster):
    return jnp.concatenate([row[:, k * cluster:(k + 1) * cluster] for k in range(row.shape[1] // cluster)], axis=0)


def split3(x):
    hi = x.astype(bf16)
    rest = x - hi.astype(f32)
    mid = rest.astype(bf16)
    low = (rest - mid.astype(f32)).astype(bf16)
    return hi, mid, low


def place(perm_row, tiles):
    count = perm_row.shape[1]
    local = lax.rem(perm_row, count)
    tile = lax.div(local, LANES)
    lane = local - tile * LANES
    at_tile = lax.broadcasted_iota(jnp.int32, (tiles, count), 0) == tile
    at_lane = lax.broadcasted_iota(jnp.int32, (LANES, count), 0) == lane
    return at_tile, jnp.where(at_lane, 1.0, 0.0).astype(bf16)


def first_deficit(state_ref, perm_ref, own_ref):
    cluster = own_ref.shape[1]
    at_tile, at_lane = place(perm_ref[...], perm_ref.shape[1] // LANES)
    deficit = to_tiles(1.0 - jnp.exp(state_ref[0:1, :])).astype(bf16)
    picked = jnp.where(at_tile, mxu(deficit, at_lane), 0.0)
    own_ref[...] = to_clusters(jnp.sum(picked, axis=0, keepdims=True), cluster)


def to_order(state_ref, friction_ref, perm_ref, fields_ref):
    cluster = fields_ref.shape[2]
    tiles = perm_ref.shape[1] // LANES
    at_tile, at_lane = place(perm_ref[...], tiles)
    coef_a, coef_b, sigma = (friction_ref[k:k + 1, :] for k in range(3))
    rows = (state_ref[0:1, :], state_ref[1:2, :], coef_a * sigma, coef_b * sigma)
    parts = [part for row in rows for part in split3(to_tiles(row))]
    moved = mxu(jnp.concatenate(parts, axis=0), at_lane)
    for k in range(len(rows)):
        three = [moved[(3 * k + s) * tiles:(3 * k + s + 1) * tiles] for s in range(3)]
        picked = jnp.where(at_tile, (three[0] + three[1]) + three[2], 0.0)
        fields_ref[k] = to_clusters(jnp.sum(picked, axis=0, keepdims=True), cluster)


def from_order(fields, perm_row, out_ref):
    tiles = perm_row.shape[1] // LANES
    at_tile, at_lane = place(perm_row, tiles)
    parts = []
    for field in fields:
        row = to_row_of_clusters(field)
        parts += [jnp.where(at_tile, part.astype(f32), 0.0).astype(bf16) for part in split3(row)]
    moved = mxu_nt(jnp.concatenate(parts, axis=0), at_lane)
    for k in range(len(fields)):
        three = [moved[(3 * k + s) * tiles:(3 * k + s + 1) * tiles] for s in range(3)]
        out_ref[k:k + 1, :] = to_row((three[0] + three[1]) + three[2])


def to_row_of_clusters(x):
    return jnp.concatenate([x[k:k + 1, :] for k in range(x.shape[0])], axis=1)


def one_hot(mask):
    return jnp.where(mask, 1.0, 0.0).astype(bf16)


def collect(mask, terms):
    hot = one_hot(mask)
    high, mid, low = split3(terms)
    return mxu(hot, high) + (mxu(hot, mid) + mxu(hot, low))


def picked(at, values):
    hot = one_hot(lax.broadcasted_iota(jnp.int32, (at.shape[0], values.shape[0]), 1) == at)
    return mxu(hot, values).astype(bf16)


def pair_terms(at, ranks, values, taken, given, wait=lambda row: None):
    pairs = at.shape[0]
    width = taken.shape[0] // pairs
    x = picked(at, values)
    shape = (PAIRS, PAIRS * width)
    rank = lax.broadcasted_iota(jnp.int32, shape, 1) - width * lax.broadcasted_iota(jnp.int32, shape, 0)
    terms = []
    for k in range(pairs // PAIRS):
        wait(k * shape[1])
        rows = slice(k * PAIRS, (k + 1) * PAIRS)
        part = pl.ds(k * shape[1], shape[1])
        within = (rank >= 0) & (rank < ranks[rows])
        coef = jnp.where(within, mxu_nt(x[rows], taken[part]), 0.0).astype(bf16)
        terms.append(mxu(coef, given[part]))
    return jnp.concatenate(terms, axis=0)


def terms_to_second(chunk, everyone_ref, near_0_ref, near_1_ref, info_ref, col_ref, left_hbm, right_hbm, kept_ref, sent_ref,
                    left, right, sem):
    copies = []
    for k in range(left.shape[0] // chunk):
        part = pl.ds(k * chunk, chunk)
        copies.append((pltpu.make_async_copy(left_hbm.at[part], left.at[part], sem.at[0, k]),
                       pltpu.make_async_copy(right_hbm.at[part], right.at[part], sem.at[1, k])))
        for copy in copies[k]:
            copy.start()

    def wait(row):
        if row % chunk == 0:
            for copy in copies[row // chunk]:
                copy.wait()

    terms = pair_terms(col_ref[:, 0:1], col_ref[:, 2:3], everyone_ref[...], left, right, wait)
    halves(sums_at(info_ref, 1, 2 * kept_ref.shape[0], terms), kept_ref, sent_ref)
    half = near_0_ref.shape[0]
    kept_ref[0:half, :] += near_0_ref[...]
    kept_ref[half:2 * half, :] += near_1_ref[...]


def terms_to_first(line_ref, more_ref, info_ref, col_ref, left, right, first_ref):
    line = jnp.concatenate([line_ref[...], more_ref[...]], axis=0).astype(bf16)
    terms = pair_terms(col_ref[:, 1:2], col_ref[:, 2:3], line, right, left)
    first_ref[...] = sums_at(info_ref, 0, first_ref.shape[0], terms).astype(bf16)


def sums_at(info_ref, side, rows, terms):
    at = lax.broadcasted_iota(jnp.int32, (rows, info_ref.shape[1]), 0) == info_ref[side:side + 1, :]
    return collect(at, terms)


def halves(x, kept_ref, sent_ref):
    step = kept_ref.shape[0]
    kept_ref[...] = x[:step]
    sent_ref[...] = x[step:].astype(sent_ref.dtype)


def join(held_ref, received_ref, out_ref):
    out_ref[...] = jnp.concatenate([held_ref[...], received_ref[...]], axis=0)


def spread(own_ref, copies_ref):
    value = own_ref[...].astype(bf16)
    for k in range(copies_ref.shape[0]):
        copies_ref[k] = value


def add(held_ref, received_ref, *out_refs):
    halves(held_ref[...] + received_ref[...], *out_refs)


HOPS = (1, 3, 7)


def place_of(difference):
    place = jnp.zeros_like(difference)
    for k in range(2 ** len(HOPS)):
        reached = 0
        for bit, hop in enumerate(HOPS):
            reached ^= hop * (k >> bit & 1)
        place = jnp.where(difference == reached, k, place)
    return place


def pair_info(own_count, columns, pairs_ref, ranks_ref, info_ref, col_ref):
    row = lax.axis_index("row")
    owner = lax.div(pairs_ref[...], own_count)
    inside = pairs_ref[...] - owner * own_count
    owner_row = lax.div(owner, columns)
    by_row = owner_row ^ row
    first_at = (owner - owner_row * columns) * own_count + inside
    second_at = place_of(by_row) * own_count + inside
    count = ranks_ref.shape[1]
    sublane = lax.broadcasted_iota(jnp.int32, (count, LANES), 0)
    lane = lax.broadcasted_iota(jnp.int32, (count, LANES), 1)
    rank = jnp.sum(jnp.where(sublane == lane, jnp.broadcast_to(ranks_ref[...], (count, LANES)), 0), axis=1, keepdims=True)
    columns_of = jnp.where(lane == 0, first_at[:, 0:1], jnp.where(lane == 1, second_at[:, 1:2], rank))
    col_ref[...] = columns_of
    info_ref[...] = jnp.transpose(columns_of)[:info_ref.shape[0]]


def near_terms(which, own_ref, near, out_ref):
    own = own_ref[...]
    half = own.shape[0] // 2
    row_own = lax.broadcasted_iota(jnp.int32, (half, own.shape[1]), 0)
    mine = own.astype(bf16)
    total = jnp.zeros(row_own.shape, f32)
    for k in range(half):
        product = mxu(mine, near[which * half + k])[which * half:(which + 1) * half]
        total += jnp.where(row_own == k, product, 0.0)
    out_ref[...] = total


def prepare(own_count, columns, pairs_ref, ranks_ref, state_ref, friction_ref, perm_ref, info_ref, col_ref, fields_ref):
    pair_info(own_count, columns, pairs_ref, ranks_ref, info_ref, col_ref)
    to_order(state_ref, friction_ref, perm_ref, fields_ref)


def slopes(lv, lt, a_sigma, b_sigma, stress):
    rate = jnp.exp(lv)
    dlt = jnp.exp(-lt) - rate
    return (stress - b_sigma * dlt) / (a_sigma + damping * rate), dlt


def total_stress(refs):
    from_first_ref, kept_ref, received_ref = refs
    parts = [from_first_ref[k].astype(f32) for k in range(from_first_ref.shape[0])]
    while len(parts) > 1:
        parts = [parts[k] + parts[k + 1] for k in range(0, len(parts), 2)]
    return parts[0] + (kept_ref[...] + received_ref[...])


def half_step(*refs):
    *stress_refs, fields_ref, slope_ref, own_ref = refs
    lv, lt, a_sigma, b_sigma = (fields_ref[k] for k in range(4))
    dlv, dlt = slopes(lv, lt, a_sigma, b_sigma, total_stress(stress_refs))
    slope_ref[0] = dlv
    slope_ref[1] = dlt
    own_ref[...] = (1.0 - jnp.exp(lv + step_size * dlv)).astype(bf16).astype(f32)


def last_step(*refs):
    *stress_refs, fields_ref, slope_ref, perm_ref, out_ref, sum_ref = refs
    lv, lt, a_sigma, b_sigma = (fields_ref[k] for k in range(4))
    first = (slope_ref[0], slope_ref[1])
    second = slopes(lv + step_size * first[0], lt + step_size * first[1], a_sigma, b_sigma, total_stress(stress_refs))
    squares = jnp.zeros(lv.shape, f32)
    news = []
    for k, base in enumerate((lv, lt)):
        new = base + 0.5 * step_size * (first[k] + second[k])
        news.append(new)
        scaled = 0.5 * step_size * (second[k] - first[k]) / (abs_tol + rel_tol * jnp.abs(new))
        squares += scaled * scaled
    sum_ref[...] = jnp.full(sum_ref.shape, jnp.sum(squares), f32)
    from_order(news, perm_ref[...], out_ref)


def in_hbm(x):
    return pltpu.with_memory_space_constraint(x, pltpu.HBM)


def call(kernel, out_shape, inputs, micros, scratch=(), streamed=()):
    many = isinstance(out_shape, (list, tuple))
    name = getattr(kernel, "func", kernel).__name__
    return pl.pallas_call(
        kernel,
        out_shape=out_shape,
        in_specs=[pl.BlockSpec(memory_space=pl.ANY) if any(x is y for y in streamed) else VMEM for x in inputs],
        out_specs=[VMEM] * len(out_shape) if many else VMEM,
        name=name,
        scratch_shapes=list(scratch),
        cost_estimate=pl.CostEstimate(flops=int(micros * 1.1e9), bytes_accessed=0, transcendentals=0),
        compiler_params=pltpu.CompilerParams(vmem_limit_bytes=32 * 1024 * 1024),
    )(*inputs)


def shards(rows, columns, state, friction, near_blocks, left_factor, right_factor, pairs, ranks, perm):
    own_count, cluster = near_blocks.shape[:2]
    count, width = left_factor.shape[:2]
    span = columns * own_count
    sds = jax.ShapeDtypeStruct
    block = sds((own_count, cluster), f32)
    perm_row = perm.reshape(1, -1)

    def swap(x, axis, distance):
        size = rows if axis == "row" else columns
        return lax.ppermute(x, axis, [(r, r ^ distance) for r in range(size)])

    own = call(first_deficit, block, [in_hbm(state), in_hbm(perm_row)], 6)
    info, info_col, fields = call(
        functools.partial(prepare, own_count, columns),
        [sds((8, count), jnp.int32), sds((count, LANES), jnp.int32), sds((4, own_count, cluster), f32)],
        [pairs, ranks.reshape(1, -1), state, friction, perm_row], 0.7)
    near = near_blocks
    left = in_hbm(left_factor.reshape(count * width, cluster))
    right = in_hbm(right_factor.reshape(count * width, cluster))

    def block_of(blocks, dtype):
        return sds((blocks * own_count, cluster), dtype)

    chunk = 2048
    scratch = [pltpu.SemaphoreType.DMA((2, count * width // chunk))]
    loaded = [pltpu.VMEM(x.shape, bf16) for x in (left, right)]

    def exchange(own):
        copies = call(spread, sds((columns, own_count, cluster), bf16), [own], 0.6)
        two = call(join, block_of(2, f32), [own, swap(own, "row", HOPS[0])], 0.1)
        four = call(join, block_of(4, f32), [two, swap(two, "row", HOPS[1])], 0.1)
        more = swap(four, "row", HOPS[2])
        everyone = lax.all_to_all(copies, "col", 0, 0).reshape(span, cluster)
        near_term = [call(functools.partial(near_terms, k), sds((own_count // 2, cluster), f32), [own, near], 0.3)
                     for k in range(2)]
        kept, sent, *factors = call(
            functools.partial(terms_to_second, chunk), [block_of(4, f32)] * 2 + loaded,
            [everyone, *near_term, info, info_col, left, right], 5, scratch, (left, right))
        first = call(terms_to_first, block_of(columns, bf16), [four, more, info, info_col, *factors], 2.5)
        for blocks, hop in ((2, HOPS[2]), (1, HOPS[1])):
            kept, sent = call(add, [block_of(blocks, f32)] * 2, [kept, swap(sent, "row", hop)], 0.1)
        from_first = lax.all_to_all(first.reshape(columns, own_count, cluster), "col", 0, 0)
        return [from_first, kept, swap(sent, "row", HOPS[0])]

    slope, own = call(half_step, [sds((2, own_count, cluster), f32), block], [*exchange(own), fields], 0.1)
    devices = rows * columns
    new_state, squares = call(last_step, [sds(state.shape, f32), sds((devices, LANES), f32)],
                              [*exchange(own), fields, slope, perm_row], 1.3)
    everywhere = lax.all_to_all(squares, ("row", "col"), 0, 0, tiled=True)
    entries = 2.0 * state.shape[1] * devices
    return new_state, jnp.sqrt(jnp.sum(everywhere[:, 0]) / entries)


def solution(mesh):
    both = ("row", "col")
    placed = (P(None, both), P(None, both), P(both, None, None), P(both, None, None), P(both, None, None),
              P(both, None), P(both), P(both))
    return jax.shard_map(
        functools.partial(shards, mesh.shape["row"], mesh.shape["col"]),
        mesh=mesh,
        in_specs=placed,
        out_specs=(P(None, both), P()),
        check_vma=False,
    )
```

```python
import functools

import jax
import jax.numpy as jnp
from jax import lax
from jax.experimental import pallas as pl
from jax.experimental.pallas import tpu as pltpu
from jax.sharding import PartitionSpec as P

step_size = 0.1
damping = 0.5
abs_tol = 0.001
rel_tol = 0.001

f32 = jnp.float32
bf16 = jnp.bfloat16
LANES = 128
PAIRS = 16
HEAD = 2048
VMEM = pl.BlockSpec(memory_space=pltpu.VMEM)


def mxu(a, b):
    return lax.dot_general(a, b, (((1,), (0,)), ((), ())), preferred_element_type=f32)


def mxu_nt(a, b):
    return lax.dot_general(a, b, (((1,), (1,)), ((), ())), preferred_element_type=f32)


def to_tiles(row):
    return jnp.concatenate([row[:, k * LANES:(k + 1) * LANES] for k in range(row.shape[1] // LANES)], axis=0)


def to_row(tiles):
    return jnp.concatenate([tiles[k:k + 1, :] for k in range(tiles.shape[0])], axis=1)


def to_clusters(row, cluster):
    return jnp.concatenate([row[:, k * cluster:(k + 1) * cluster] for k in range(row.shape[1] // cluster)], axis=0)


def split3(x):
    hi = x.astype(bf16)
    rest = x - hi.astype(f32)
    mid = rest.astype(bf16)
    low = (rest - mid.astype(f32)).astype(bf16)
    return hi, mid, low


def place(perm_row, tiles):
    count = perm_row.shape[1]
    local = lax.rem(perm_row, count)
    tile = lax.div(local, LANES)
    lane = local - tile * LANES
    at_tile = lax.broadcasted_iota(jnp.int32, (tiles, count), 0) == tile
    at_lane = lax.broadcasted_iota(jnp.int32, (LANES, count), 0) == lane
    return at_tile, jnp.where(at_lane, 1.0, 0.0).astype(bf16)


def first_deficit(state_ref, perm_ref, own_ref):
    cluster = own_ref.shape[1]
    at_tile, at_lane = place(perm_ref[...], perm_ref.shape[1] // LANES)
    deficit = to_tiles(1.0 - jnp.exp(state_ref[0:1, :])).astype(bf16)
    picked = jnp.where(at_tile, mxu(deficit, at_lane), 0.0)
    own_ref[...] = to_clusters(jnp.sum(picked, axis=0, keepdims=True), cluster)


def to_order(state_ref, friction_ref, perm_ref, fields_ref):
    cluster = fields_ref.shape[2]
    tiles = perm_ref.shape[1] // LANES
    at_tile, at_lane = place(perm_ref[...], tiles)
    coef_a, coef_b, sigma = (friction_ref[k:k + 1, :] for k in range(3))
    rows = (state_ref[0:1, :], state_ref[1:2, :], coef_a * sigma, coef_b * sigma)
    parts = [part for row in rows for part in split3(to_tiles(row))]
    moved = mxu(jnp.concatenate(parts, axis=0), at_lane)
    for k in range(len(rows)):
        three = [moved[(3 * k + s) * tiles:(3 * k + s + 1) * tiles] for s in range(3)]
        picked = jnp.where(at_tile, (three[0] + three[1]) + three[2], 0.0)
        fields_ref[k] = to_clusters(jnp.sum(picked, axis=0, keepdims=True), cluster)


def from_order(fields, perm_row, out_ref):
    tiles = perm_row.shape[1] // LANES
    at_tile, at_lane = place(perm_row, tiles)
    parts = []
    for field in fields:
        row = to_row_of_clusters(field)
        parts += [jnp.where(at_tile, part.astype(f32), 0.0).astype(bf16) for part in split3(row)]
    moved = mxu_nt(jnp.concatenate(parts, axis=0), at_lane)
    for k in range(len(fields)):
        three = [moved[(3 * k + s) * tiles:(3 * k + s + 1) * tiles] for s in range(3)]
        out_ref[k:k + 1, :] = to_row((three[0] + three[1]) + three[2])


def to_row_of_clusters(x):
    return jnp.concatenate([x[k:k + 1, :] for k in range(x.shape[0])], axis=1)


def one_hot(mask):
    return jnp.where(mask, 1.0, 0.0).astype(bf16)


def collect(mask, terms):
    hot = one_hot(mask)
    high = terms.astype(bf16)
    return mxu(hot, high) + mxu(hot, (terms - high.astype(f32)).astype(bf16))


def picked(at, values):
    hot = one_hot(lax.broadcasted_iota(jnp.int32, (at.shape[0], values.shape[0]), 1) == at)
    return mxu(hot, values).astype(bf16)


def pair_terms(at, ranks, values, taken, given):
    x = picked(at, values)
    groups = at.shape[0] // PAIRS
    coefs = []
    for k in range(groups):
        factor = taken(k)
        shape = (PAIRS, factor.shape[0])
        rank = lax.broadcasted_iota(jnp.int32, shape, 1) - shape[1] // PAIRS * lax.broadcasted_iota(jnp.int32, shape, 0)
        rows = slice(k * PAIRS, (k + 1) * PAIRS)
        within = (rank >= 0) & (rank < ranks[rows])
        coefs.append(jnp.where(within, mxu_nt(x[rows], factor), 0.0).astype(bf16))
    return jnp.concatenate([mxu(coefs[k], given(k)) for k in range(groups)], axis=0)


def part_of(k, rows, head, tail):
    first = head.shape[0] // rows
    return head[pl.ds(k * rows, rows)] if k < first else tail[pl.ds((k - first) * rows, rows)]


def second_sums(chunk, everyone_ref, near_0_ref, near_1_ref, info_ref, col_ref, sources, heads, tails, sem, load_heads,
                kept_ref, sent_ref):
    pairs = info_ref.shape[1]
    rows = (heads[0].shape[0] + tails[0].shape[0]) // pairs * PAIRS
    fetched = []
    for which, (source, head, tail) in enumerate(zip(sources, heads, tails)):
        start = head.shape[0]
        copies = {}
        if load_heads:
            copies[0] = pltpu.make_async_copy(source.at[pl.ds(0, start)], head, sem.at[which, 0])
        for k in range(tail.shape[0] // chunk):
            part, at = pl.ds(k * chunk, chunk), start + k * chunk
            copies[at] = pltpu.make_async_copy(source.at[pl.ds(at, chunk)], tail.at[part], sem.at[which, k + 1])
        for copy in copies.values():
            copy.start()

        def group(k, head=head, tail=tail, copies=copies):
            if k * rows in copies:
                copies[k * rows].wait()
            return part_of(k, rows, head, tail)

        fetched.append(group)
    terms = pair_terms(col_ref[:, 0:1], col_ref[:, 2:3], everyone_ref[...], *fetched)
    halves(sums_at(info_ref, 1, 2 * kept_ref.shape[0], terms), kept_ref, sent_ref)
    half = near_0_ref.shape[0]
    kept_ref[0:half, :] += near_0_ref[...]
    kept_ref[half:2 * half, :] += near_1_ref[...]


def terms_to_second(chunk, everyone, near_0, near_1, info, col, left_hbm, right_hbm, kept, sent, left_head, right_head,
                    left, right, sem):
    second_sums(chunk, everyone, near_0, near_1, info, col, (left_hbm, right_hbm), (left_head, right_head), (left, right),
                sem, True, kept, sent)


def terms_to_second_again(chunk, everyone, near_0, near_1, info, col, left_head, right_head, left_hbm, right_hbm, kept, sent,
                          left, right, sem):
    second_sums(chunk, everyone, near_0, near_1, info, col, (left_hbm, right_hbm), (left_head, right_head), (left, right),
                sem, False, kept, sent)


def terms_to_first(line_ref, more_ref, info_ref, col_ref, left_head, right_head, left, right, first_ref):
    line = jnp.concatenate([line_ref[...], more_ref[...]], axis=0).astype(bf16)
    rows = (left_head.shape[0] + left.shape[0]) // info_ref.shape[1] * PAIRS
    terms = pair_terms(col_ref[:, 1:2], col_ref[:, 2:3], line, lambda k: part_of(k, rows, right_head, right),
                       lambda k: part_of(k, rows, left_head, left))
    first_ref[...] = sums_at(info_ref, 0, first_ref.shape[0], terms).astype(bf16)


def sums_at(info_ref, side, rows, terms):
    at = lax.broadcasted_iota(jnp.int32, (rows, info_ref.shape[1]), 0) == info_ref[side:side + 1, :]
    return collect(at, terms)


def halves(x, kept_ref, sent_ref):
    step = kept_ref.shape[0]
    kept_ref[...] = x[:step]
    sent_ref[...] = x[step:].astype(sent_ref.dtype)


def join(held_ref, received_ref, out_ref):
    out_ref[...] = jnp.concatenate([held_ref[...], received_ref[...]], axis=0)


def spread(own_ref, copies_ref):
    value = own_ref[...].astype(bf16)
    for k in range(copies_ref.shape[0]):
        copies_ref[k] = value


def add(held_ref, received_ref, *out_refs):
    halves(held_ref[...] + received_ref[...], *out_refs)


HOPS = (1, 3, 7)


def place_of(difference):
    place = jnp.zeros_like(difference)
    for k in range(2 ** len(HOPS)):
        reached = 0
        for bit, hop in enumerate(HOPS):
            reached ^= hop * (k >> bit & 1)
        place = jnp.where(difference == reached, k, place)
    return place


def pair_info(own_count, columns, pairs_ref, ranks_ref, info_ref, col_ref):
    row = lax.axis_index("row")
    owner = lax.div(pairs_ref[...], own_count)
    inside = pairs_ref[...] - owner * own_count
    owner_row = lax.div(owner, columns)
    by_row = owner_row ^ row
    first_at = (owner - owner_row * columns) * own_count + inside
    second_at = place_of(by_row) * own_count + inside
    count = ranks_ref.shape[1]
    sublane = lax.broadcasted_iota(jnp.int32, (count, LANES), 0)
    lane = lax.broadcasted_iota(jnp.int32, (count, LANES), 1)
    rank = jnp.sum(jnp.where(sublane == lane, jnp.broadcast_to(ranks_ref[...], (count, LANES)), 0), axis=1, keepdims=True)
    columns_of = jnp.where(lane == 0, first_at[:, 0:1], jnp.where(lane == 1, second_at[:, 1:2], rank))
    col_ref[...] = columns_of
    info_ref[...] = jnp.transpose(columns_of)[:info_ref.shape[0]]


def near_terms(which, two_ref, near, out_ref):
    half = out_ref.shape[0]
    row_own = lax.broadcasted_iota(jnp.int32, out_ref.shape, 0)
    mine = two_ref[0:2 * half, :].astype(bf16)
    total = jnp.zeros(row_own.shape, f32)
    for k in range(half):
        product = mxu(mine, near[which * half + k])[which * half:(which + 1) * half]
        total += jnp.where(row_own == k, product, 0.0)
    out_ref[...] = total


def prepare(own_count, columns, _, pairs_ref, ranks_ref, state_ref, friction_ref, perm_ref, info_ref, col_ref, fields_ref):
    pair_info(own_count, columns, pairs_ref, ranks_ref, info_ref, col_ref)
    to_order(state_ref, friction_ref, perm_ref, fields_ref)


def slopes(lv, lt, a_sigma, b_sigma, stress):
    rate = jnp.exp(lv)
    dlt = jnp.exp(-lt) - rate
    return (stress - b_sigma * dlt) / (a_sigma + damping * rate), dlt


def total_stress(refs):
    from_first_ref, kept_ref, received_ref = refs
    parts = [from_first_ref[k].astype(f32) for k in range(from_first_ref.shape[0])]
    while len(parts) > 1:
        parts = [parts[k] + parts[k + 1] for k in range(0, len(parts), 2)]
    return parts[0] + (kept_ref[...] + received_ref[...])


def half_step(*refs):
    *stress_refs, fields_ref, slope_ref, own_ref = refs
    lv, lt, a_sigma, b_sigma = (fields_ref[k] for k in range(4))
    dlv, dlt = slopes(lv, lt, a_sigma, b_sigma, total_stress(stress_refs))
    slope_ref[0] = dlv
    slope_ref[1] = dlt
    own_ref[...] = (1.0 - jnp.exp(lv + step_size * dlv)).astype(bf16).astype(f32)


def last_step(*refs):
    *stress_refs, fields_ref, slope_ref, perm_ref, out_ref, sum_ref = refs
    lv, lt, a_sigma, b_sigma = (fields_ref[k] for k in range(4))
    first = (slope_ref[0], slope_ref[1])
    second = slopes(lv + step_size * first[0], lt + step_size * first[1], a_sigma, b_sigma, total_stress(stress_refs))
    squares = jnp.zeros(lv.shape, f32)
    news = []
    for k, base in enumerate((lv, lt)):
        new = base + 0.5 * step_size * (first[k] + second[k])
        news.append(new)
        scaled = 0.5 * step_size * (second[k] - first[k]) / (abs_tol + rel_tol * jnp.abs(new))
        squares += scaled * scaled
    sum_ref[...] = jnp.full(sum_ref.shape, jnp.sum(squares), f32)
    from_order(news, perm_ref[...], out_ref)


def in_hbm(x):
    return pltpu.with_memory_space_constraint(x, pltpu.HBM)


def call(kernel, out_shape, inputs, micros, scratch=(), streamed=()):
    many = isinstance(out_shape, (list, tuple))
    name = getattr(kernel, "func", kernel).__name__
    return pl.pallas_call(
        kernel,
        out_shape=out_shape,
        in_specs=[pl.BlockSpec(memory_space=pl.ANY) if any(x is y for y in streamed) else VMEM for x in inputs],
        out_specs=[VMEM] * len(out_shape) if many else VMEM,
        name=name,
        scratch_shapes=list(scratch),
        cost_estimate=pl.CostEstimate(flops=int(micros * 1.1e9), bytes_accessed=0, transcendentals=0),
        compiler_params=pltpu.CompilerParams(vmem_limit_bytes=32 * 1024 * 1024),
    )(*inputs)


def shards(rows, columns, state, friction, near_blocks, left_factor, right_factor, pairs, ranks, perm):
    own_count, cluster = near_blocks.shape[:2]
    count, width = left_factor.shape[:2]
    span = columns * own_count
    sds = jax.ShapeDtypeStruct
    block = sds((own_count, cluster), f32)
    perm_row = perm.reshape(1, -1)

    def swap(x, axis, distance):
        size = rows if axis == "row" else columns
        return lax.ppermute(x, axis, [(r, r ^ distance) for r in range(size)])

    own = call(first_deficit, block, [in_hbm(state), in_hbm(perm_row)], 6)
    near = near_blocks
    left = in_hbm(left_factor.reshape(count * width, cluster))
    right = in_hbm(right_factor.reshape(count * width, cluster))

    def block_of(blocks, dtype):
        return sds((blocks * own_count, cluster), dtype)

    chunk, head = 2048, HEAD
    tail = count * width - head
    scratch = [pltpu.SemaphoreType.DMA((2, tail // chunk + 1))]
    kept_there = [pltpu.VMEM((head, cluster), bf16)] * 2
    loaded = [pltpu.VMEM((tail, cluster), bf16)] * 2

    def exchange(own, prepared=None, heads=None):
        copies = call(spread, sds((columns, own_count, cluster), bf16), [own], 0.6)
        two = call(join, block_of(2, f32), [own, swap(own, "row", HOPS[0])], 0.1)
        if prepared is None:
            prepared = call(
                functools.partial(prepare, own_count, columns),
                [sds((8, count), jnp.int32), sds((count, LANES), jnp.int32), sds((4, own_count, cluster), f32)],
                [two, pairs, ranks.reshape(1, -1), state, friction, perm_row], 0.7)
        info, info_col, _ = prepared
        four = call(join, block_of(4, f32), [two, swap(two, "row", HOPS[1])], 0.1)
        more = swap(four, "row", HOPS[2])
        everyone = lax.all_to_all(copies, "col", 0, 0).reshape(span, cluster)
        near_term = [call(functools.partial(near_terms, k), sds((own_count // 2, cluster), f32), [two, near], 0.3)
                     for k in range(2)]
        if heads is None:
            kept, sent, *factors = call(
                functools.partial(terms_to_second, chunk), [block_of(4, f32)] * 2 + kept_there + loaded,
                [everyone, *near_term, info, info_col, left, right], 5, scratch, (left, right))
            heads, factors = factors[:2], factors[2:]
        else:
            kept, sent, *factors = call(
                functools.partial(terms_to_second_again, chunk), [block_of(4, f32)] * 2 + loaded,
                [everyone, *near_term, info, info_col, *heads, left, right], 5, scratch, (left, right))
        first = call(terms_to_first, block_of(columns, bf16), [four, more, info, info_col, *heads, *factors], 2.5)
        for blocks, hop in ((2, HOPS[2]), (1, HOPS[1])):
            kept, sent = call(add, [block_of(blocks, f32)] * 2, [kept, swap(sent, "row", hop)], 0.1)
        from_first = lax.all_to_all(first.reshape(columns, own_count, cluster), "col", 0, 0)
        return [from_first, kept, swap(sent, "row", HOPS[0])], prepared, heads

    received, prepared, heads = exchange(own)
    fields = prepared[2]
    slope, own = call(half_step, [sds((2, own_count, cluster), f32), block], [*received, fields], 0.1)
    received, _, _ = exchange(own, prepared, heads)
    devices = rows * columns
    new_state, squares = call(last_step, [sds(state.shape, f32), sds((devices, LANES), f32)],
                              [*received, fields, slope, perm_row], 1.3)
    everywhere = lax.all_to_all(squares, ("row", "col"), 0, 0, tiled=True)
    entries = 2.0 * state.shape[1] * devices
    return new_state, jnp.sqrt(jnp.sum(everywhere[:, 0]) / entries)


def solution(mesh):
    both = ("row", "col")
    placed = (P(None, both), P(None, both), P(both, None, None), P(both, None, None), P(both, None, None),
              P(both, None), P(both), P(both))
    return jax.shard_map(
        functools.partial(shards, mesh.shape["row"], mesh.shape["col"]),
        mesh=mesh,
        in_specs=placed,
        out_specs=(P(None, both), P()),
        check_vma=False,
    )
```

```python
import functools

import jax
import jax.numpy as jnp
from jax import lax
from jax.experimental import pallas as pl
from jax.experimental.pallas import tpu as pltpu
from jax.sharding import PartitionSpec as P

step_size = 0.1
damping = 0.5
abs_tol = 0.001
rel_tol = 0.001

f32 = jnp.float32
bf16 = jnp.bfloat16
LANES = 128
PAIRS = 16
HEAD = 2048
VMEM = pl.BlockSpec(memory_space=pltpu.VMEM)


def mxu(a, b):
    return lax.dot_general(a, b, (((1,), (0,)), ((), ())), preferred_element_type=f32)


def mxu_nt(a, b):
    return lax.dot_general(a, b, (((1,), (1,)), ((), ())), preferred_element_type=f32)


def to_tiles(row):
    return jnp.concatenate([row[:, k * LANES:(k + 1) * LANES] for k in range(row.shape[1] // LANES)], axis=0)


def to_row(tiles):
    return jnp.concatenate([tiles[k:k + 1, :] for k in range(tiles.shape[0])], axis=1)


def to_clusters(row, cluster):
    return jnp.concatenate([row[:, k * cluster:(k + 1) * cluster] for k in range(row.shape[1] // cluster)], axis=0)


def split3(x):
    hi = x.astype(bf16)
    rest = x - hi.astype(f32)
    mid = rest.astype(bf16)
    low = (rest - mid.astype(f32)).astype(bf16)
    return hi, mid, low


def place(perm_row, tiles):
    count = perm_row.shape[1]
    local = lax.rem(perm_row, count)
    tile = lax.div(local, LANES)
    lane = local - tile * LANES
    at_tile = lax.broadcasted_iota(jnp.int32, (tiles, count), 0) == tile
    at_lane = lax.broadcasted_iota(jnp.int32, (LANES, count), 0) == lane
    return at_tile, jnp.where(at_lane, 1.0, 0.0).astype(bf16)


def first_deficit(state_ref, perm_ref, own_ref):
    cluster = own_ref.shape[1]
    at_tile, at_lane = place(perm_ref[...], perm_ref.shape[1] // LANES)
    deficit = to_tiles(1.0 - jnp.exp(state_ref[0:1, :])).astype(bf16)
    picked = jnp.where(at_tile, mxu(deficit, at_lane), 0.0)
    own_ref[...] = to_clusters(jnp.sum(picked, axis=0, keepdims=True), cluster)


def to_order(state_ref, friction_ref, perm_ref, fields_ref):
    cluster = fields_ref.shape[2]
    tiles = perm_ref.shape[1] // LANES
    at_tile, at_lane = place(perm_ref[...], tiles)
    coef_a, coef_b, sigma = (friction_ref[k:k + 1, :] for k in range(3))
    rows = (state_ref[0:1, :], state_ref[1:2, :], coef_a * sigma, coef_b * sigma)
    parts = [part for row in rows for part in split3(to_tiles(row))]
    moved = mxu(jnp.concatenate(parts, axis=0), at_lane)
    for k in range(len(rows)):
        three = [moved[(3 * k + s) * tiles:(3 * k + s + 1) * tiles] for s in range(3)]
        picked = jnp.where(at_tile, (three[0] + three[1]) + three[2], 0.0)
        fields_ref[k] = to_clusters(jnp.sum(picked, axis=0, keepdims=True), cluster)


def from_order(fields, perm_row, out_ref):
    tiles = perm_row.shape[1] // LANES
    at_tile, at_lane = place(perm_row, tiles)
    parts = []
    for field in fields:
        row = to_row_of_clusters(field)
        parts += [jnp.where(at_tile, part.astype(f32), 0.0).astype(bf16) for part in split3(row)]
    moved = mxu_nt(jnp.concatenate(parts, axis=0), at_lane)
    for k in range(len(fields)):
        three = [moved[(3 * k + s) * tiles:(3 * k + s + 1) * tiles] for s in range(3)]
        out_ref[k:k + 1, :] = to_row((three[0] + three[1]) + three[2])


def to_row_of_clusters(x):
    return jnp.concatenate([x[k:k + 1, :] for k in range(x.shape[0])], axis=1)


def one_hot(mask):
    return jnp.where(mask, 1.0, 0.0).astype(bf16)


def collect(mask, terms):
    hot = one_hot(mask)
    high = terms.astype(bf16)
    return mxu(hot, high) + mxu(hot, (terms - high.astype(f32)).astype(bf16))


def picked(at, values):
    hot = one_hot(lax.broadcasted_iota(jnp.int32, (at.shape[0], values.shape[0]), 1) == at)
    return mxu(hot, values).astype(bf16)


def pair_terms(at, ranks, values, taken, given):
    x = picked(at, values)
    groups = at.shape[0] // PAIRS
    coefs = []
    for k in range(groups):
        factor = taken(k)
        shape = (PAIRS, factor.shape[0])
        rank = lax.broadcasted_iota(jnp.int32, shape, 1) - shape[1] // PAIRS * lax.broadcasted_iota(jnp.int32, shape, 0)
        rows = slice(k * PAIRS, (k + 1) * PAIRS)
        within = (rank >= 0) & (rank < ranks[rows])
        coefs.append(jnp.where(within, mxu_nt(x[rows], factor), 0.0).astype(bf16))
    return jnp.concatenate([mxu(coefs[k], given(k)) for k in range(groups)], axis=0)


def part_of(k, rows, head, tail):
    first = head.shape[0] // rows
    return head[pl.ds(k * rows, rows)] if k < first else tail[pl.ds((k - first) * rows, rows)]


def second_sums(chunk, everyone_ref, near_0_ref, near_1_ref, info_ref, col_ref, sources, heads, tails, sem, load_heads,
                kept_ref, sent_ref):
    pairs = info_ref.shape[1]
    rows = (heads[0].shape[0] + tails[0].shape[0]) // pairs * PAIRS
    fetched = []
    for which, (source, head, tail) in enumerate(zip(sources, heads, tails)):
        start = head.shape[0]
        copies = {}
        if load_heads:
            copies[0] = pltpu.make_async_copy(source.at[pl.ds(0, start)], head, sem.at[which, 0])
        for k in range(tail.shape[0] // chunk):
            part, at = pl.ds(k * chunk, chunk), start + k * chunk
            copies[at] = pltpu.make_async_copy(source.at[pl.ds(at, chunk)], tail.at[part], sem.at[which, k + 1])
        for copy in copies.values():
            copy.start()

        def group(k, head=head, tail=tail, copies=copies):
            if k * rows in copies:
                copies[k * rows].wait()
            return part_of(k, rows, head, tail)

        fetched.append(group)
    terms = pair_terms(col_ref[:, 0:1], col_ref[:, 2:3], everyone_ref[...], *fetched)
    halves(sums_at(info_ref, 1, 2 * kept_ref.shape[0], terms), kept_ref, sent_ref)
    half = near_0_ref.shape[0]
    kept_ref[0:half, :] += near_0_ref[...]
    kept_ref[half:2 * half, :] += near_1_ref[...]


def terms_to_second(chunk, everyone, near_0, near_1, info, col, left_hbm, right_hbm, kept, sent, left_head, right_head,
                    left, right, sem):
    second_sums(chunk, everyone, near_0, near_1, info, col, (left_hbm, right_hbm), (left_head, right_head), (left, right),
                sem, True, kept, sent)


def terms_to_second_again(chunk, everyone, near_0, near_1, info, col, left_head, right_head, left_hbm, right_hbm, kept, sent,
                          left, right, sem):
    second_sums(chunk, everyone, near_0, near_1, info, col, (left_hbm, right_hbm), (left_head, right_head), (left, right),
                sem, False, kept, sent)


def terms_to_first(line_ref, more_ref, info_ref, col_ref, left_head, right_head, left, right, first_ref):
    line = jnp.concatenate([line_ref[...], more_ref[...]], axis=0).astype(bf16)
    rows = (left_head.shape[0] + left.shape[0]) // info_ref.shape[1] * PAIRS
    terms = pair_terms(col_ref[:, 1:2], col_ref[:, 2:3], line, lambda k: part_of(k, rows, right_head, right),
                       lambda k: part_of(k, rows, left_head, left))
    first_ref[...] = sums_at(info_ref, 0, first_ref.shape[0], terms).astype(bf16)


def sums_at(info_ref, side, rows, terms):
    at = lax.broadcasted_iota(jnp.int32, (rows, info_ref.shape[1]), 0) == info_ref[side:side + 1, :]
    return collect(at, terms)


def halves(x, kept_ref, sent_ref):
    step = kept_ref.shape[0]
    kept_ref[...] = x[:step]
    sent_ref[...] = x[step:].astype(sent_ref.dtype)


def join(held_ref, received_ref, out_ref):
    out_ref[...] = jnp.concatenate([held_ref[...], received_ref[...]], axis=0)


def spread(own_ref, copies_ref):
    value = own_ref[...].astype(bf16)
    for k in range(copies_ref.shape[0]):
        copies_ref[k] = value


def add(held_ref, received_ref, *out_refs):
    halves(held_ref[...] + received_ref[...], *out_refs)


HOPS = (1, 3, 7)


def place_of(difference):
    place = jnp.zeros_like(difference)
    for k in range(2 ** len(HOPS)):
        reached = 0
        for bit, hop in enumerate(HOPS):
            reached ^= hop * (k >> bit & 1)
        place = jnp.where(difference == reached, k, place)
    return place


def pair_info(own_count, columns, pairs_ref, ranks_ref, info_ref, col_ref):
    row = lax.axis_index("row")
    owner = lax.div(pairs_ref[...], own_count)
    inside = pairs_ref[...] - owner * own_count
    owner_row = lax.div(owner, columns)
    by_row = owner_row ^ row
    first_at = (owner - owner_row * columns) * own_count + inside
    second_at = place_of(by_row) * own_count + inside
    count = ranks_ref.shape[1]
    sublane = lax.broadcasted_iota(jnp.int32, (count, LANES), 0)
    lane = lax.broadcasted_iota(jnp.int32, (count, LANES), 1)
    rank = jnp.sum(jnp.where(sublane == lane, jnp.broadcast_to(ranks_ref[...], (count, LANES)), 0), axis=1, keepdims=True)
    columns_of = jnp.where(lane == 0, first_at[:, 0:1], jnp.where(lane == 1, second_at[:, 1:2], rank))
    col_ref[...] = columns_of
    info_ref[...] = jnp.transpose(columns_of)[:info_ref.shape[0]]


def near_terms(which, two_ref, near, out_ref):
    half = out_ref.shape[0]
    row_own = lax.broadcasted_iota(jnp.int32, out_ref.shape, 0)
    mine = two_ref[0:2 * half, :].astype(bf16)
    total = jnp.zeros(row_own.shape, f32)
    for k in range(half):
        product = mxu(mine, near[which * half + k])[which * half:(which + 1) * half]
        total += jnp.where(row_own == k, product, 0.0)
    out_ref[...] = total


def prepare(own_count, columns, _, pairs_ref, ranks_ref, state_ref, friction_ref, perm_ref, info_ref, col_ref, fields_ref):
    pair_info(own_count, columns, pairs_ref, ranks_ref, info_ref, col_ref)
    to_order(state_ref, friction_ref, perm_ref, fields_ref)


def slopes(lv, lt, a_sigma, b_sigma, stress):
    rate = jnp.exp(lv)
    dlt = jnp.exp(-lt) - rate
    return (stress - b_sigma * dlt) / (a_sigma + damping * rate), dlt


def total_stress(refs):
    from_first_ref, kept_ref, received_ref = refs
    parts = [from_first_ref[k].astype(f32) for k in range(from_first_ref.shape[0])]
    while len(parts) > 1:
        parts = [parts[k] + parts[k + 1] for k in range(0, len(parts), 2)]
    return parts[0] + (kept_ref[...] + received_ref[...])


def half_step(*refs):
    *stress_refs, fields_ref, slope_ref, own_ref = refs
    lv, lt, a_sigma, b_sigma = (fields_ref[k] for k in range(4))
    dlv, dlt = slopes(lv, lt, a_sigma, b_sigma, total_stress(stress_refs))
    slope_ref[0] = dlv
    slope_ref[1] = dlt
    own_ref[...] = (1.0 - jnp.exp(lv + step_size * dlv)).astype(bf16).astype(f32)


def last_step(*refs):
    *stress_refs, fields_ref, slope_ref, new_ref, sum_ref = refs
    lv, lt, a_sigma, b_sigma = (fields_ref[k] for k in range(4))
    first = (slope_ref[0], slope_ref[1])
    second = slopes(lv + step_size * first[0], lt + step_size * first[1], a_sigma, b_sigma, total_stress(stress_refs))
    squares = jnp.zeros(lv.shape, f32)
    for k, base in enumerate((lv, lt)):
        new = base + 0.5 * step_size * (first[k] + second[k])
        new_ref[k] = new
        scaled = 0.5 * step_size * (second[k] - first[k]) / (abs_tol + rel_tol * jnp.abs(new))
        squares += scaled * scaled
    sum_ref[...] = jnp.full(sum_ref.shape, jnp.sum(squares), f32)


def finish(entries, everywhere_ref, new_ref, perm_ref, out_ref, norm_ref):
    norm_ref[...] = jnp.sqrt(jnp.sum(everywhere_ref[...], axis=0, keepdims=True)[:, 0:1] / entries)
    from_order([new_ref[0], new_ref[1]], perm_ref[...], out_ref)


def in_hbm(x):
    return pltpu.with_memory_space_constraint(x, pltpu.HBM)


def call(kernel, out_shape, inputs, micros, scratch=(), streamed=()):
    many = isinstance(out_shape, (list, tuple))
    name = getattr(kernel, "func", kernel).__name__
    return pl.pallas_call(
        kernel,
        out_shape=out_shape,
        in_specs=[pl.BlockSpec(memory_space=pl.ANY) if any(x is y for y in streamed) else VMEM for x in inputs],
        out_specs=[VMEM] * len(out_shape) if many else VMEM,
        name=name,
        scratch_shapes=list(scratch),
        cost_estimate=pl.CostEstimate(flops=int(micros * 1.1e9), bytes_accessed=0, transcendentals=0),
        compiler_params=pltpu.CompilerParams(vmem_limit_bytes=32 * 1024 * 1024),
    )(*inputs)


def shards(rows, columns, state, friction, near_blocks, left_factor, right_factor, pairs, ranks, perm):
    own_count, cluster = near_blocks.shape[:2]
    count, width = left_factor.shape[:2]
    span = columns * own_count
    sds = jax.ShapeDtypeStruct
    block = sds((own_count, cluster), f32)
    perm_row = perm.reshape(1, -1)

    def swap(x, axis, distance):
        size = rows if axis == "row" else columns
        return lax.ppermute(x, axis, [(r, r ^ distance) for r in range(size)])

    own = call(first_deficit, block, [in_hbm(state), in_hbm(perm_row)], 6)
    near = near_blocks
    left = in_hbm(left_factor.reshape(count * width, cluster))
    right = in_hbm(right_factor.reshape(count * width, cluster))

    def block_of(blocks, dtype):
        return sds((blocks * own_count, cluster), dtype)

    chunk, head = 2048, HEAD
    tail = count * width - head
    scratch = [pltpu.SemaphoreType.DMA((2, tail // chunk + 1))]
    kept_there = [pltpu.VMEM((head, cluster), bf16)] * 2
    loaded = [pltpu.VMEM((tail, cluster), bf16)] * 2

    def exchange(own, prepared=None, heads=None):
        copies = call(spread, sds((columns, own_count, cluster), bf16), [own], 0.6)
        two = call(join, block_of(2, f32), [own, swap(own, "row", HOPS[0])], 0.1)
        if prepared is None:
            prepared = call(
                functools.partial(prepare, own_count, columns),
                [sds((8, count), jnp.int32), sds((count, LANES), jnp.int32), sds((4, own_count, cluster), f32)],
                [two, pairs, ranks.reshape(1, -1), state, friction, perm_row], 0.7)
        info, info_col, _ = prepared
        four = call(join, block_of(4, f32), [two, swap(two, "row", HOPS[1])], 0.1)
        more = swap(four, "row", HOPS[2])
        everyone = lax.all_to_all(copies, "col", 0, 0).reshape(span, cluster)
        near_term = [call(functools.partial(near_terms, k), sds((own_count // 2, cluster), f32), [two, near], 0.3)
                     for k in range(2)]
        if heads is None:
            kept, sent, *factors = call(
                functools.partial(terms_to_second, chunk), [block_of(4, f32)] * 2 + kept_there + loaded,
                [everyone, *near_term, info, info_col, left, right], 5, scratch, (left, right))
            heads, factors = factors[:2], factors[2:]
        else:
            kept, sent, *factors = call(
                functools.partial(terms_to_second_again, chunk), [block_of(4, f32)] * 2 + loaded,
                [everyone, *near_term, info, info_col, *heads, left, right], 5, scratch, (left, right))
        first = call(terms_to_first, block_of(columns, bf16), [four, more, info, info_col, *heads, *factors], 2.5)
        for blocks, hop in ((2, HOPS[2]), (1, HOPS[1])):
            kept, sent = call(add, [block_of(blocks, f32)] * 2, [kept, swap(sent, "row", hop)], 0.1)
        from_first = lax.all_to_all(first.reshape(columns, own_count, cluster), "col", 0, 0)
        return [from_first, kept, swap(sent, "row", HOPS[0])], prepared, heads

    received, prepared, heads = exchange(own)
    fields = prepared[2]
    slope, own = call(half_step, [sds((2, own_count, cluster), f32), block], [*received, fields], 0.1)
    received, _, _ = exchange(own, prepared, heads)
    devices = rows * columns
    new, squares = call(last_step, [sds((2, own_count, cluster), f32), sds((devices, LANES), f32)],
                        [*received, fields, slope], 0.2)
    everywhere = lax.all_to_all(squares, ("row", "col"), 0, 0, tiled=True)
    entries = 2.0 * state.shape[1] * devices
    new_state, norm = call(functools.partial(finish, entries), [sds(state.shape, f32), sds((1, 1), f32)],
                           [everywhere, new, perm_row], 1)
    return new_state, norm.reshape(())


def solution(mesh):
    both = ("row", "col")
    placed = (P(None, both), P(None, both), P(both, None, None), P(both, None, None), P(both, None, None),
              P(both, None), P(both), P(both))
    return jax.shard_map(
        functools.partial(shards, mesh.shape["row"], mesh.shape["col"]),
        mesh=mesh,
        in_specs=placed,
        out_specs=(P(None, both), P()),
        check_vma=False,
    )
```

```python
import functools

import jax
import jax.numpy as jnp
from jax import lax
from jax.experimental import pallas as pl
from jax.experimental.pallas import tpu as pltpu
from jax.sharding import PartitionSpec as P

step_size = 0.1
damping = 0.5
abs_tol = 0.001
rel_tol = 0.001

f32 = jnp.float32
bf16 = jnp.bfloat16
LANES = 128
PAIRS = 16
HEAD = 2048
VMEM = pl.BlockSpec(memory_space=pltpu.VMEM)


def mxu(a, b):
    return lax.dot_general(a, b, (((1,), (0,)), ((), ())), preferred_element_type=f32)


def mxu_nt(a, b):
    return lax.dot_general(a, b, (((1,), (1,)), ((), ())), preferred_element_type=f32)


def to_tiles(row):
    return jnp.concatenate([row[:, k * LANES:(k + 1) * LANES] for k in range(row.shape[1] // LANES)], axis=0)


def to_row(tiles):
    return jnp.concatenate([tiles[k:k + 1, :] for k in range(tiles.shape[0])], axis=1)


def to_clusters(row, cluster):
    return jnp.concatenate([row[:, k * cluster:(k + 1) * cluster] for k in range(row.shape[1] // cluster)], axis=0)


def split3(x):
    hi = x.astype(bf16)
    rest = x - hi.astype(f32)
    mid = rest.astype(bf16)
    low = (rest - mid.astype(f32)).astype(bf16)
    return hi, mid, low


def place(perm_row, tiles):
    count = perm_row.shape[1]
    local = lax.rem(perm_row, count)
    tile = lax.div(local, LANES)
    lane = local - tile * LANES
    at_tile = lax.broadcasted_iota(jnp.int32, (tiles, count), 0) == tile
    at_lane = lax.broadcasted_iota(jnp.int32, (LANES, count), 0) == lane
    return at_tile, jnp.where(at_lane, 1.0, 0.0).astype(bf16)


def first_deficit(state_ref, perm_ref, own_ref):
    cluster = own_ref.shape[1]
    at_tile, at_lane = place(perm_ref[...], perm_ref.shape[1] // LANES)
    deficit = to_tiles(1.0 - jnp.exp(state_ref[0:1, :])).astype(bf16)
    picked = jnp.where(at_tile, mxu(deficit, at_lane), 0.0)
    own_ref[...] = to_clusters(jnp.sum(picked, axis=0, keepdims=True), cluster)


def to_order(state_ref, friction_ref, perm_ref, fields_ref):
    cluster = fields_ref.shape[2]
    tiles = perm_ref.shape[1] // LANES
    at_tile, at_lane = place(perm_ref[...], tiles)
    coef_a, coef_b, sigma = (friction_ref[k:k + 1, :] for k in range(3))
    rows = (state_ref[0:1, :], state_ref[1:2, :], coef_a * sigma, coef_b * sigma)
    parts = [part for row in rows for part in split3(to_tiles(row))]
    moved = mxu(jnp.concatenate(parts, axis=0), at_lane)
    for k in range(len(rows)):
        three = [moved[(3 * k + s) * tiles:(3 * k + s + 1) * tiles] for s in range(3)]
        picked = jnp.where(at_tile, (three[0] + three[1]) + three[2], 0.0)
        fields_ref[k] = to_clusters(jnp.sum(picked, axis=0, keepdims=True), cluster)


def from_order(fields, perm_row, out_ref):
    tiles = perm_row.shape[1] // LANES
    at_tile, at_lane = place(perm_row, tiles)
    parts = []
    for field in fields:
        row = to_row_of_clusters(field)
        parts += [jnp.where(at_tile, part.astype(f32), 0.0).astype(bf16) for part in split3(row)]
    moved = mxu_nt(jnp.concatenate(parts, axis=0), at_lane)
    for k in range(len(fields)):
        three = [moved[(3 * k + s) * tiles:(3 * k + s + 1) * tiles] for s in range(3)]
        out_ref[k:k + 1, :] = to_row((three[0] + three[1]) + three[2])


def to_row_of_clusters(x):
    return jnp.concatenate([x[k:k + 1, :] for k in range(x.shape[0])], axis=1)


def one_hot(mask):
    return jnp.where(mask, 1.0, 0.0).astype(bf16)


def collect(mask, terms):
    hot = one_hot(mask)
    high = terms.astype(bf16)
    return mxu(hot, high) + mxu(hot, (terms - high.astype(f32)).astype(bf16))


def picked(at, values):
    hot = one_hot(lax.broadcasted_iota(jnp.int32, (at.shape[0], values.shape[0]), 1) == at)
    return mxu(hot, values).astype(bf16)


def pair_terms(at, ranks, values, taken, given):
    x = picked(at, values)
    groups = at.shape[0] // PAIRS
    coefs = []
    for k in range(groups):
        factor = taken(k)
        shape = (PAIRS, factor.shape[0])
        rank = lax.broadcasted_iota(jnp.int32, shape, 1) - shape[1] // PAIRS * lax.broadcasted_iota(jnp.int32, shape, 0)
        rows = slice(k * PAIRS, (k + 1) * PAIRS)
        within = (rank >= 0) & (rank < ranks[rows])
        coefs.append(jnp.where(within, mxu_nt(x[rows], factor), 0.0).astype(bf16))
    return jnp.concatenate([mxu(coefs[k], given(k)) for k in range(groups)], axis=0)


def part_of(k, rows, head, tail):
    first = head.shape[0] // rows
    return head[pl.ds(k * rows, rows)] if k < first else tail[pl.ds((k - first) * rows, rows)]


def second_sums(chunk, everyone_ref, near_0_ref, near_1_ref, info_ref, col_ref, sources, heads, tails, sem, load_heads,
                kept_ref, sent_ref):
    pairs = info_ref.shape[1]
    rows = (heads[0].shape[0] + tails[0].shape[0]) // pairs * PAIRS
    fetched = []
    for which, (source, head, tail) in enumerate(zip(sources, heads, tails)):
        start = head.shape[0]
        copies = {}
        if load_heads:
            copies[0] = pltpu.make_async_copy(source.at[pl.ds(0, start)], head, sem.at[which, 0])
        for k in range(tail.shape[0] // chunk):
            part, at = pl.ds(k * chunk, chunk), start + k * chunk
            copies[at] = pltpu.make_async_copy(source.at[pl.ds(at, chunk)], tail.at[part], sem.at[which, k + 1])
        for copy in copies.values():
            copy.start()

        def group(k, head=head, tail=tail, copies=copies):
            if k * rows in copies:
                copies[k * rows].wait()
            return part_of(k, rows, head, tail)

        fetched.append(group)
    terms = pair_terms(col_ref[:, 0:1], col_ref[:, 2:3], everyone_ref[...], *fetched)
    halves(sums_at(info_ref, 1, 2 * kept_ref.shape[0], terms), kept_ref, sent_ref)
    half = near_0_ref.shape[0]
    kept_ref[0:half, :] += near_0_ref[...]
    kept_ref[half:2 * half, :] += near_1_ref[...]


def terms_to_second(chunk, everyone, near_0, near_1, info, col, left_hbm, right_hbm, kept, sent, left_head, right_head,
                    left, right, sem):
    second_sums(chunk, everyone, near_0, near_1, info, col, (left_hbm, right_hbm), (left_head, right_head), (left, right),
                sem, True, kept, sent)


def terms_to_second_again(chunk, everyone, near_0, near_1, info, col, left_head, right_head, left_hbm, right_hbm, kept, sent,
                          left, right, sem):
    second_sums(chunk, everyone, near_0, near_1, info, col, (left_hbm, right_hbm), (left_head, right_head), (left, right),
                sem, False, kept, sent)


def terms_to_first(line_ref, more_ref, info_ref, col_ref, left_head, right_head, left, right, first_ref):
    line = jnp.concatenate([line_ref[...], more_ref[...]], axis=0).astype(bf16)
    rows = (left_head.shape[0] + left.shape[0]) // info_ref.shape[1] * PAIRS
    terms = pair_terms(col_ref[:, 1:2], col_ref[:, 2:3], line, lambda k: part_of(k, rows, right_head, right),
                       lambda k: part_of(k, rows, left_head, left))
    first_ref[...] = sums_at(info_ref, 0, first_ref.shape[0], terms)


def sums_at(info_ref, side, rows, terms):
    at = lax.broadcasted_iota(jnp.int32, (rows, info_ref.shape[1]), 0) == info_ref[side:side + 1, :]
    return collect(at, terms)


def halves(x, kept_ref, sent_ref):
    step = kept_ref.shape[0]
    kept_ref[...] = x[:step]
    sent_ref[...] = x[step:].astype(sent_ref.dtype)


def join(held_ref, received_ref, out_ref):
    out_ref[...] = jnp.concatenate([held_ref[...], received_ref[...]], axis=0)


def spread(own_ref, copies_ref):
    value = own_ref[...].astype(bf16)
    for k in range(copies_ref.shape[0]):
        copies_ref[k] = value


def add(held_ref, received_ref, *out_refs):
    halves(held_ref[...] + received_ref[...], *out_refs)


HOPS = (1, 3, 7)


def place_of(difference):
    place = jnp.zeros_like(difference)
    for k in range(2 ** len(HOPS)):
        reached = 0
        for bit, hop in enumerate(HOPS):
            reached ^= hop * (k >> bit & 1)
        place = jnp.where(difference == reached, k, place)
    return place


def pair_info(own_count, columns, pairs_ref, ranks_ref, info_ref, col_ref):
    row = lax.axis_index("row")
    owner = lax.div(pairs_ref[...], own_count)
    inside = pairs_ref[...] - owner * own_count
    owner_row = lax.div(owner, columns)
    by_row = owner_row ^ row
    first_at = (owner - owner_row * columns) * own_count + inside
    second_at = place_of(by_row) * own_count + inside
    count = ranks_ref.shape[1]
    sublane = lax.broadcasted_iota(jnp.int32, (count, LANES), 0)
    lane = lax.broadcasted_iota(jnp.int32, (count, LANES), 1)
    rank = jnp.sum(jnp.where(sublane == lane, jnp.broadcast_to(ranks_ref[...], (count, LANES)), 0), axis=1, keepdims=True)
    columns_of = jnp.where(lane == 0, first_at[:, 0:1], jnp.where(lane == 1, second_at[:, 1:2], rank))
    col_ref[...] = columns_of
    info_ref[...] = jnp.transpose(columns_of)[:info_ref.shape[0]]


def near_terms(which, two_ref, near, out_ref):
    half = out_ref.shape[0]
    row_own = lax.broadcasted_iota(jnp.int32, out_ref.shape, 0)
    mine = two_ref[0:2 * half, :].astype(bf16)
    total = jnp.zeros(row_own.shape, f32)
    for k in range(half):
        product = mxu(mine, near[which * half + k])[which * half:(which + 1) * half]
        total += jnp.where(row_own == k, product, 0.0)
    out_ref[...] = total


def prepare(own_count, columns, _, pairs_ref, ranks_ref, state_ref, friction_ref, perm_ref, info_ref, col_ref, fields_ref):
    pair_info(own_count, columns, pairs_ref, ranks_ref, info_ref, col_ref)
    to_order(state_ref, friction_ref, perm_ref, fields_ref)


def slopes(lv, lt, a_sigma, b_sigma, stress):
    rate = jnp.exp(lv)
    dlt = jnp.exp(-lt) - rate
    return (stress - b_sigma * dlt) / (a_sigma + damping * rate), dlt


def total_stress(refs):
    from_first_ref, kept_ref, received_ref = refs
    parts = [from_first_ref[k] for k in range(from_first_ref.shape[0])]
    while len(parts) > 1:
        parts = [parts[k] + parts[k + 1] for k in range(0, len(parts), 2)]
    return parts[0] + (kept_ref[...] + received_ref[...])


def half_step(*refs):
    *stress_refs, fields_ref, slope_ref, own_ref = refs
    lv, lt, a_sigma, b_sigma = (fields_ref[k] for k in range(4))
    dlv, dlt = slopes(lv, lt, a_sigma, b_sigma, total_stress(stress_refs))
    slope_ref[0] = dlv
    slope_ref[1] = dlt
    own_ref[...] = (1.0 - jnp.exp(lv + step_size * dlv)).astype(bf16).astype(f32)


def last_step(*refs):
    *stress_refs, fields_ref, slope_ref, new_ref, sum_ref = refs
    lv, lt, a_sigma, b_sigma = (fields_ref[k] for k in range(4))
    first = (slope_ref[0], slope_ref[1])
    second = slopes(lv + step_size * first[0], lt + step_size * first[1], a_sigma, b_sigma, total_stress(stress_refs))
    squares = jnp.zeros(lv.shape, f32)
    for k, base in enumerate((lv, lt)):
        new = base + 0.5 * step_size * (first[k] + second[k])
        new_ref[k] = new
        scaled = 0.5 * step_size * (second[k] - first[k]) / (abs_tol + rel_tol * jnp.abs(new))
        squares += scaled * scaled
    sum_ref[...] = jnp.full(sum_ref.shape, jnp.sum(squares), f32)


def finish(entries, everywhere_ref, new_ref, perm_ref, out_ref, norm_ref):
    norm_ref[...] = jnp.sqrt(jnp.sum(everywhere_ref[...], axis=0, keepdims=True)[:, 0:1] / entries)
    from_order([new_ref[0], new_ref[1]], perm_ref[...], out_ref)


def in_hbm(x):
    return pltpu.with_memory_space_constraint(x, pltpu.HBM)


def call(kernel, out_shape, inputs, micros, scratch=(), streamed=()):
    many = isinstance(out_shape, (list, tuple))
    name = getattr(kernel, "func", kernel).__name__
    return pl.pallas_call(
        kernel,
        out_shape=out_shape,
        in_specs=[pl.BlockSpec(memory_space=pl.ANY) if any(x is y for y in streamed) else VMEM for x in inputs],
        out_specs=[VMEM] * len(out_shape) if many else VMEM,
        name=name,
        scratch_shapes=list(scratch),
        cost_estimate=pl.CostEstimate(flops=int(micros * 1.1e9), bytes_accessed=0, transcendentals=0),
        compiler_params=pltpu.CompilerParams(vmem_limit_bytes=32 * 1024 * 1024),
    )(*inputs)


def shards(rows, columns, state, friction, near_blocks, left_factor, right_factor, pairs, ranks, perm):
    own_count, cluster = near_blocks.shape[:2]
    count, width = left_factor.shape[:2]
    span = columns * own_count
    sds = jax.ShapeDtypeStruct
    block = sds((own_count, cluster), f32)
    perm_row = perm.reshape(1, -1)

    def swap(x, axis, distance):
        size = rows if axis == "row" else columns
        return lax.ppermute(x, axis, [(r, r ^ distance) for r in range(size)])

    own = call(first_deficit, block, [in_hbm(state), in_hbm(perm_row)], 6)
    near = near_blocks
    left = in_hbm(left_factor.reshape(count * width, cluster))
    right = in_hbm(right_factor.reshape(count * width, cluster))

    def block_of(blocks, dtype):
        return sds((blocks * own_count, cluster), dtype)

    chunk, head = 2048, HEAD
    tail = count * width - head
    scratch = [pltpu.SemaphoreType.DMA((2, tail // chunk + 1))]
    kept_there = [pltpu.VMEM((head, cluster), bf16)] * 2
    loaded = [pltpu.VMEM((tail, cluster), bf16)] * 2

    def exchange(own, prepared=None, heads=None):
        copies = call(spread, sds((columns, own_count, cluster), bf16), [own], 0.6)
        two = call(join, block_of(2, f32), [own, swap(own, "row", HOPS[0])], 0.1)
        if prepared is None:
            prepared = call(
                functools.partial(prepare, own_count, columns),
                [sds((8, count), jnp.int32), sds((count, LANES), jnp.int32), sds((4, own_count, cluster), f32)],
                [two, pairs, ranks.reshape(1, -1), state, friction, perm_row], 0.7)
        info, info_col, _ = prepared
        four = call(join, block_of(4, f32), [two, swap(two, "row", HOPS[1])], 0.1)
        more = swap(four, "row", HOPS[2])
        everyone = lax.all_to_all(copies, "col", 0, 0).reshape(span, cluster)
        near_term = [call(functools.partial(near_terms, k), sds((own_count // 2, cluster), f32), [two, near], 0.3)
                     for k in range(2)]
        if heads is None:
            kept, sent, *factors = call(
                functools.partial(terms_to_second, chunk), [block_of(4, f32)] * 2 + kept_there + loaded,
                [everyone, *near_term, info, info_col, left, right], 5, scratch, (left, right))
            heads, factors = factors[:2], factors[2:]
        else:
            kept, sent, *factors = call(
                functools.partial(terms_to_second_again, chunk), [block_of(4, f32)] * 2 + loaded,
                [everyone, *near_term, info, info_col, *heads, left, right], 5, scratch, (left, right))
        first = call(terms_to_first, block_of(columns, f32), [four, more, info, info_col, *heads, *factors], 2.5)
        for blocks, hop, cost in ((2, HOPS[2], 1.0), (1, HOPS[1], 0.1)):
            kept, sent = call(add, [block_of(blocks, f32)] * 2, [kept, swap(sent, "row", hop)], cost)
        from_first = lax.all_to_all(first.reshape(columns, own_count, cluster), "col", 0, 0)
        return [from_first, kept, swap(sent, "row", HOPS[0])], prepared, heads

    received, prepared, heads = exchange(own)
    fields = prepared[2]
    slope, own = call(half_step, [sds((2, own_count, cluster), f32), block], [*received, fields], 0.1)
    received, _, _ = exchange(own, prepared, heads)
    devices = rows * columns
    new, squares = call(last_step, [sds((2, own_count, cluster), f32), sds((devices, LANES), f32)],
                        [*received, fields, slope], 0.2)
    everywhere = lax.all_to_all(squares, ("row", "col"), 0, 0, tiled=True)
    entries = 2.0 * state.shape[1] * devices
    new_state, norm = call(functools.partial(finish, entries), [sds(state.shape, f32), sds((1, 1), f32)],
                           [everywhere, new, perm_row], 1)
    return new_state, norm.reshape(())


def solution(mesh):
    both = ("row", "col")
    placed = (P(None, both), P(None, both), P(both, None, None), P(both, None, None), P(both, None, None),
              P(both, None), P(both), P(both))
    return jax.shard_map(
        functools.partial(shards, mesh.shape["row"], mesh.shape["col"]),
        mesh=mesh,
        in_specs=placed,
        out_specs=(P(None, both), P()),
        check_vma=False,
    )
```

```python
import functools

import jax
import jax.numpy as jnp
from jax import lax
from jax.experimental import pallas as pl
from jax.experimental.pallas import tpu as pltpu
from jax.sharding import PartitionSpec as P

step_size = 0.1
damping = 0.5
abs_tol = 0.001
rel_tol = 0.001

f32 = jnp.float32
bf16 = jnp.bfloat16
LANES = 128
PAIRS = 16
HEAD = 2048
VMEM = pl.BlockSpec(memory_space=pltpu.VMEM)


def mxu(a, b):
    return lax.dot_general(a, b, (((1,), (0,)), ((), ())), preferred_element_type=f32)


def mxu_nt(a, b):
    return lax.dot_general(a, b, (((1,), (1,)), ((), ())), preferred_element_type=f32)


def to_tiles(row):
    return jnp.concatenate([row[:, k * LANES:(k + 1) * LANES] for k in range(row.shape[1] // LANES)], axis=0)


def to_row(tiles):
    return jnp.concatenate([tiles[k:k + 1, :] for k in range(tiles.shape[0])], axis=1)


def to_clusters(row, cluster):
    return jnp.concatenate([row[:, k * cluster:(k + 1) * cluster] for k in range(row.shape[1] // cluster)], axis=0)


def split3(x):
    hi = x.astype(bf16)
    rest = x - hi.astype(f32)
    mid = rest.astype(bf16)
    low = (rest - mid.astype(f32)).astype(bf16)
    return hi, mid, low


def place(perm_row, tiles):
    count = perm_row.shape[1]
    local = lax.rem(perm_row, count)
    tile = lax.div(local, LANES)
    lane = local - tile * LANES
    at_tile = lax.broadcasted_iota(jnp.int32, (tiles, count), 0) == tile
    at_lane = lax.broadcasted_iota(jnp.int32, (LANES, count), 0) == lane
    return at_tile, jnp.where(at_lane, 1.0, 0.0).astype(bf16)


def first_deficit(state_ref, perm_ref, own_ref):
    cluster = own_ref.shape[1]
    at_tile, at_lane = place(perm_ref[...], perm_ref.shape[1] // LANES)
    deficit = to_tiles(1.0 - jnp.exp(state_ref[0:1, :])).astype(bf16)
    picked = jnp.where(at_tile, mxu(deficit, at_lane), 0.0)
    own_ref[...] = to_clusters(jnp.sum(picked, axis=0, keepdims=True), cluster)


def to_order(state_ref, friction_ref, perm_ref, fields_ref):
    cluster = fields_ref.shape[2]
    tiles = perm_ref.shape[1] // LANES
    at_tile, at_lane = place(perm_ref[...], tiles)
    coef_a, coef_b, sigma = (friction_ref[k:k + 1, :] for k in range(3))
    rows = (state_ref[0:1, :], state_ref[1:2, :], coef_a * sigma, coef_b * sigma)
    parts = [part for row in rows for part in split3(to_tiles(row))]
    moved = mxu(jnp.concatenate(parts, axis=0), at_lane)
    for k in range(len(rows)):
        three = [moved[(3 * k + s) * tiles:(3 * k + s + 1) * tiles] for s in range(3)]
        picked = jnp.where(at_tile, (three[0] + three[1]) + three[2], 0.0)
        fields_ref[k] = to_clusters(jnp.sum(picked, axis=0, keepdims=True), cluster)


def from_order(fields, perm_row, out_ref):
    tiles = perm_row.shape[1] // LANES
    at_tile, at_lane = place(perm_row, tiles)
    parts = []
    for field in fields:
        row = to_row_of_clusters(field)
        parts += [jnp.where(at_tile, part.astype(f32), 0.0).astype(bf16) for part in split3(row)]
    moved = mxu_nt(jnp.concatenate(parts, axis=0), at_lane)
    for k in range(len(fields)):
        three = [moved[(3 * k + s) * tiles:(3 * k + s + 1) * tiles] for s in range(3)]
        out_ref[k:k + 1, :] = to_row((three[0] + three[1]) + three[2])


def to_row_of_clusters(x):
    return jnp.concatenate([x[k:k + 1, :] for k in range(x.shape[0])], axis=1)


def one_hot(mask):
    return jnp.where(mask, 1.0, 0.0).astype(bf16)


def collect(mask, terms):
    hot = one_hot(mask)
    high = terms.astype(bf16)
    return mxu(hot, high) + mxu(hot, (terms - high.astype(f32)).astype(bf16))


def picked(at, values):
    hot = one_hot(lax.broadcasted_iota(jnp.int32, (at.shape[0], values.shape[0]), 1) == at)
    return mxu(hot, values).astype(bf16)


def pair_terms(at, ranks, values, product, given):
    x = picked(at, values)
    groups = at.shape[0] // PAIRS
    coefs = []
    for k in range(groups):
        rows = slice(k * PAIRS, (k + 1) * PAIRS)
        coef = product(x[rows], k)
        shape = coef.shape
        rank = lax.broadcasted_iota(jnp.int32, shape, 1) - shape[1] // PAIRS * lax.broadcasted_iota(jnp.int32, shape, 0)
        within = (rank >= 0) & (rank < ranks[rows])
        coefs.append(jnp.where(within, coef, 0.0).astype(bf16))
    return jnp.concatenate([mxu(coefs[k], given(k)) for k in range(groups)], axis=0)


def part_of(k, rows, head, tail):
    first = head.shape[0] // rows
    return head[pl.ds(k * rows, rows)] if k < first else tail[pl.ds((k - first) * rows, rows)]


def second_sums(chunk, everyone_ref, near_0_ref, near_1_ref, info_ref, col_ref, sources, heads, tails, sem, load_heads,
                kept_ref, sent_ref, right_t):
    pairs = info_ref.shape[1]
    rows = (heads[0].shape[0] + tails[0].shape[0]) // pairs * PAIRS
    fetched = []
    for which, (source, head, tail) in enumerate(zip(sources, heads, tails)):
        start = head.shape[0]
        copies = {}
        if load_heads:
            copies[0] = pltpu.make_async_copy(source.at[pl.ds(0, start)], head, sem.at[which, 0])
        for k in range(tail.shape[0] // chunk):
            part, at = pl.ds(k * chunk, chunk), start + k * chunk
            copies[at] = pltpu.make_async_copy(source.at[pl.ds(at, chunk)], tail.at[part], sem.at[which, k + 1])
        for copy in copies.values():
            copy.start()

        def group(k, head=head, tail=tail, copies=copies):
            if k * rows in copies:
                copies[k * rows].wait()
            return part_of(k, rows, head, tail)

        fetched.append(group)
    left_rows, right_rows = fetched

    def transposing(k):
        right = right_rows(k)
        right_t[:, pl.ds(k * rows, rows)] = jnp.transpose(right)
        return right

    terms = pair_terms(col_ref[:, 0:1], col_ref[:, 2:3], everyone_ref[...], lambda x, k: mxu_nt(x, left_rows(k)), transposing)
    halves(sums_at(info_ref, 1, 2 * kept_ref.shape[0], terms), kept_ref, sent_ref)
    half = near_0_ref.shape[0]
    kept_ref[0:half, :] += near_0_ref[...]
    kept_ref[half:2 * half, :] += near_1_ref[...]


def terms_to_second(chunk, everyone, near_0, near_1, info, col, left_hbm, right_hbm, kept, sent, left_head, right_head,
                    left, right_t, right, sem):
    second_sums(chunk, everyone, near_0, near_1, info, col, (left_hbm, right_hbm), (left_head, right_head), (left, right),
                sem, True, kept, sent, right_t)


def terms_to_second_again(chunk, everyone, near_0, near_1, info, col, left_head, right_head, left_hbm, right_hbm, kept, sent,
                          left, right_t, right, sem):
    second_sums(chunk, everyone, near_0, near_1, info, col, (left_hbm, right_hbm), (left_head, right_head), (left, right),
                sem, False, kept, sent, right_t)


def terms_to_first(line_ref, more_ref, info_ref, col_ref, left_head, left, right_t, first_ref):
    line = jnp.concatenate([line_ref[...], more_ref[...]], axis=0).astype(bf16)
    rows = right_t.shape[1] // info_ref.shape[1] * PAIRS
    terms = pair_terms(col_ref[:, 1:2], col_ref[:, 2:3], line, lambda x, k: mxu(x, right_t[:, pl.ds(k * rows, rows)]),
                       lambda k: part_of(k, rows, left_head, left))
    first_ref[...] = sums_at(info_ref, 0, first_ref.shape[0], terms)


def sums_at(info_ref, side, rows, terms):
    at = lax.broadcasted_iota(jnp.int32, (rows, info_ref.shape[1]), 0) == info_ref[side:side + 1, :]
    return collect(at, terms)


def halves(x, kept_ref, sent_ref):
    step = kept_ref.shape[0]
    kept_ref[...] = x[:step]
    sent_ref[...] = x[step:].astype(sent_ref.dtype)


def join(held_ref, received_ref, out_ref):
    out_ref[...] = jnp.concatenate([held_ref[...], received_ref[...]], axis=0)


def spread(own_ref, copies_ref):
    value = own_ref[...].astype(bf16)
    for k in range(copies_ref.shape[0]):
        copies_ref[k] = value


def add(held_ref, received_ref, *out_refs):
    halves(held_ref[...] + received_ref[...], *out_refs)


HOPS = (1, 3, 7)


def place_of(difference):
    place = jnp.zeros_like(difference)
    for k in range(2 ** len(HOPS)):
        reached = 0
        for bit, hop in enumerate(HOPS):
            reached ^= hop * (k >> bit & 1)
        place = jnp.where(difference == reached, k, place)
    return place


def pair_info(own_count, columns, pairs_ref, ranks_ref, info_ref, col_ref):
    row = lax.axis_index("row")
    owner = lax.div(pairs_ref[...], own_count)
    inside = pairs_ref[...] - owner * own_count
    owner_row = lax.div(owner, columns)
    by_row = owner_row ^ row
    first_at = (owner - owner_row * columns) * own_count + inside
    second_at = place_of(by_row) * own_count + inside
    count = ranks_ref.shape[1]
    sublane = lax.broadcasted_iota(jnp.int32, (count, LANES), 0)
    lane = lax.broadcasted_iota(jnp.int32, (count, LANES), 1)
    rank = jnp.sum(jnp.where(sublane == lane, jnp.broadcast_to(ranks_ref[...], (count, LANES)), 0), axis=1, keepdims=True)
    columns_of = jnp.where(lane == 0, first_at[:, 0:1], jnp.where(lane == 1, second_at[:, 1:2], rank))
    col_ref[...] = columns_of
    info_ref[...] = jnp.transpose(columns_of)[:info_ref.shape[0]]


def near_terms(which, two_ref, near, out_ref):
    half = out_ref.shape[0]
    row_own = lax.broadcasted_iota(jnp.int32, out_ref.shape, 0)
    mine = two_ref[0:2 * half, :].astype(bf16)
    total = jnp.zeros(row_own.shape, f32)
    for k in range(half):
        product = mxu(mine, near[which * half + k])[which * half:(which + 1) * half]
        total += jnp.where(row_own == k, product, 0.0)
    out_ref[...] = total


def prepare(own_count, columns, _, pairs_ref, ranks_ref, state_ref, friction_ref, perm_ref, info_ref, col_ref, fields_ref):
    pair_info(own_count, columns, pairs_ref, ranks_ref, info_ref, col_ref)
    to_order(state_ref, friction_ref, perm_ref, fields_ref)


def slopes(lv, lt, a_sigma, b_sigma, stress):
    rate = jnp.exp(lv)
    dlt = jnp.exp(-lt) - rate
    return (stress - b_sigma * dlt) / (a_sigma + damping * rate), dlt


def total_stress(refs):
    from_first_ref, kept_ref, received_ref = refs
    parts = [from_first_ref[k] for k in range(from_first_ref.shape[0])]
    while len(parts) > 1:
        parts = [parts[k] + parts[k + 1] for k in range(0, len(parts), 2)]
    return parts[0] + (kept_ref[...] + received_ref[...])


def half_step(*refs):
    *stress_refs, fields_ref, slope_ref, own_ref = refs
    lv, lt, a_sigma, b_sigma = (fields_ref[k] for k in range(4))
    dlv, dlt = slopes(lv, lt, a_sigma, b_sigma, total_stress(stress_refs))
    slope_ref[0] = dlv
    slope_ref[1] = dlt
    own_ref[...] = (1.0 - jnp.exp(lv + step_size * dlv)).astype(bf16).astype(f32)


def last_step(*refs):
    *stress_refs, fields_ref, slope_ref, new_ref, sum_ref = refs
    lv, lt, a_sigma, b_sigma = (fields_ref[k] for k in range(4))
    first = (slope_ref[0], slope_ref[1])
    second = slopes(lv + step_size * first[0], lt + step_size * first[1], a_sigma, b_sigma, total_stress(stress_refs))
    squares = jnp.zeros(lv.shape, f32)
    for k, base in enumerate((lv, lt)):
        new = base + 0.5 * step_size * (first[k] + second[k])
        new_ref[k] = new
        scaled = 0.5 * step_size * (second[k] - first[k]) / (abs_tol + rel_tol * jnp.abs(new))
        squares += scaled * scaled
    sum_ref[...] = jnp.full(sum_ref.shape, jnp.sum(squares), f32)


def finish(entries, everywhere_ref, new_ref, perm_ref, out_ref, norm_ref):
    norm_ref[...] = jnp.sqrt(jnp.sum(everywhere_ref[...], axis=0, keepdims=True)[:, 0:1] / entries)
    from_order([new_ref[0], new_ref[1]], perm_ref[...], out_ref)


def in_hbm(x):
    return pltpu.with_memory_space_constraint(x, pltpu.HBM)


def call(kernel, out_shape, inputs, micros, scratch=(), streamed=()):
    many = isinstance(out_shape, (list, tuple))
    name = getattr(kernel, "func", kernel).__name__
    return pl.pallas_call(
        kernel,
        out_shape=out_shape,
        in_specs=[pl.BlockSpec(memory_space=pl.ANY) if any(x is y for y in streamed) else VMEM for x in inputs],
        out_specs=[VMEM] * len(out_shape) if many else VMEM,
        name=name,
        scratch_shapes=list(scratch),
        cost_estimate=pl.CostEstimate(flops=int(micros * 1.1e9), bytes_accessed=0, transcendentals=0),
        compiler_params=pltpu.CompilerParams(vmem_limit_bytes=32 * 1024 * 1024),
    )(*inputs)


def shards(rows, columns, state, friction, near_blocks, left_factor, right_factor, pairs, ranks, perm):
    own_count, cluster = near_blocks.shape[:2]
    count, width = left_factor.shape[:2]
    span = columns * own_count
    sds = jax.ShapeDtypeStruct
    block = sds((own_count, cluster), f32)
    perm_row = perm.reshape(1, -1)

    def swap(x, axis, distance):
        size = rows if axis == "row" else columns
        return lax.ppermute(x, axis, [(r, r ^ distance) for r in range(size)])

    own = call(first_deficit, block, [in_hbm(state), in_hbm(perm_row)], 6)
    near = near_blocks
    left = in_hbm(left_factor.reshape(count * width, cluster))
    right = in_hbm(right_factor.reshape(count * width, cluster))

    def block_of(blocks, dtype):
        return sds((blocks * own_count, cluster), dtype)

    chunk, head = 2048, HEAD
    tail = count * width - head
    scratch = [pltpu.VMEM((tail, cluster), bf16), pltpu.SemaphoreType.DMA((2, tail // chunk + 1))]
    kept_there = [pltpu.VMEM((head, cluster), bf16)] * 2
    loaded = [pltpu.VMEM((tail, cluster), bf16), pltpu.VMEM((cluster, count * width), bf16)]

    def exchange(own, prepared=None, heads=None):
        copies = call(spread, sds((columns, own_count, cluster), bf16), [own], 0.6)
        two = call(join, block_of(2, f32), [own, swap(own, "row", HOPS[0])], 0.1)
        if prepared is None:
            prepared = call(
                functools.partial(prepare, own_count, columns),
                [sds((8, count), jnp.int32), sds((count, LANES), jnp.int32), sds((4, own_count, cluster), f32)],
                [two, pairs, ranks.reshape(1, -1), state, friction, perm_row], 0.7)
        info, info_col, _ = prepared
        four = call(join, block_of(4, f32), [two, swap(two, "row", HOPS[1])], 0.1)
        more = swap(four, "row", HOPS[2])
        everyone = lax.all_to_all(copies, "col", 0, 0).reshape(span, cluster)
        near_term = [call(functools.partial(near_terms, k), sds((own_count // 2, cluster), f32), [two, near], 0.3)
                     for k in range(2)]
        if heads is None:
            kept, sent, *factors = call(
                functools.partial(terms_to_second, chunk), [block_of(4, f32)] * 2 + kept_there + loaded,
                [everyone, *near_term, info, info_col, left, right], 5, scratch, (left, right))
            heads, factors = factors[:2], factors[2:]
        else:
            kept, sent, *factors = call(
                functools.partial(terms_to_second_again, chunk), [block_of(4, f32)] * 2 + loaded,
                [everyone, *near_term, info, info_col, *heads, left, right], 5, scratch, (left, right))
        first = call(terms_to_first, block_of(columns, f32), [four, more, info, info_col, heads[0], *factors], 2.5)
        for blocks, hop, cost in ((2, HOPS[2], 1.0), (1, HOPS[1], 0.1)):
            kept, sent = call(add, [block_of(blocks, f32)] * 2, [kept, swap(sent, "row", hop)], cost)
        from_first = lax.all_to_all(first.reshape(columns, own_count, cluster), "col", 0, 0)
        return [from_first, kept, swap(sent, "row", HOPS[0])], prepared, heads

    received, prepared, heads = exchange(own)
    fields = prepared[2]
    slope, own = call(half_step, [sds((2, own_count, cluster), f32), block], [*received, fields], 0.1)
    received, _, _ = exchange(own, prepared, heads)
    devices = rows * columns
    new, squares = call(last_step, [sds((2, own_count, cluster), f32), sds((devices, LANES), f32)],
                        [*received, fields, slope], 0.2)
    everywhere = lax.all_to_all(squares, ("row", "col"), 0, 0, tiled=True)
    entries = 2.0 * state.shape[1] * devices
    new_state, norm = call(functools.partial(finish, entries), [sds(state.shape, f32), sds((1, 1), f32)],
                           [everywhere, new, perm_row], 1)
    return new_state, norm.reshape(())


def solution(mesh):
    both = ("row", "col")
    placed = (P(None, both), P(None, both), P(both, None, None), P(both, None, None), P(both, None, None),
              P(both, None), P(both), P(both))
    return jax.shard_map(
        functools.partial(shards, mesh.shape["row"], mesh.shape["col"]),
        mesh=mesh,
        in_specs=placed,
        out_specs=(P(None, both), P()),
        check_vma=False,
    )
```

```python
import functools

import jax
import jax.numpy as jnp
from jax import lax
from jax.experimental import pallas as pl
from jax.experimental.pallas import tpu as pltpu
from jax.sharding import PartitionSpec as P

step_size = 0.1
damping = 0.5
abs_tol = 0.001
rel_tol = 0.001

f32 = jnp.float32
bf16 = jnp.bfloat16
LANES = 128
PAIRS = 16
HEAD = 2048
VMEM = pl.BlockSpec(memory_space=pltpu.VMEM)


def mxu(a, b):
    return lax.dot_general(a, b, (((1,), (0,)), ((), ())), preferred_element_type=f32)


def mxu_nt(a, b):
    return lax.dot_general(a, b, (((1,), (1,)), ((), ())), preferred_element_type=f32)


def to_tiles(row):
    return jnp.concatenate([row[:, k * LANES:(k + 1) * LANES] for k in range(row.shape[1] // LANES)], axis=0)


def to_row(tiles):
    return jnp.concatenate([tiles[k:k + 1, :] for k in range(tiles.shape[0])], axis=1)


def to_clusters(row, cluster):
    return jnp.concatenate([row[:, k * cluster:(k + 1) * cluster] for k in range(row.shape[1] // cluster)], axis=0)


def split3(x):
    hi = x.astype(bf16)
    rest = x - hi.astype(f32)
    mid = rest.astype(bf16)
    low = (rest - mid.astype(f32)).astype(bf16)
    return hi, mid, low


def place(perm_row, tiles):
    count = perm_row.shape[1]
    local = lax.rem(perm_row, count)
    tile = lax.div(local, LANES)
    lane = local - tile * LANES
    at_tile = lax.broadcasted_iota(jnp.int32, (tiles, count), 0) == tile
    at_lane = lax.broadcasted_iota(jnp.int32, (LANES, count), 0) == lane
    return at_tile, jnp.where(at_lane, 1.0, 0.0).astype(bf16)


def first_deficit(state_ref, perm_ref, own_ref):
    cluster = own_ref.shape[1]
    at_tile, at_lane = place(perm_ref[...], perm_ref.shape[1] // LANES)
    deficit = to_tiles(1.0 - jnp.exp(state_ref[0:1, :])).astype(bf16)
    picked = jnp.where(at_tile, mxu(deficit, at_lane), 0.0)
    own_ref[...] = to_clusters(jnp.sum(picked, axis=0, keepdims=True), cluster)


def to_order(state_ref, friction_ref, perm_ref, fields_ref):
    cluster = fields_ref.shape[2]
    tiles = perm_ref.shape[1] // LANES
    at_tile, at_lane = place(perm_ref[...], tiles)
    coef_a, coef_b, sigma = (friction_ref[k:k + 1, :] for k in range(3))
    rows = (state_ref[0:1, :], state_ref[1:2, :], coef_a * sigma, coef_b * sigma)
    parts = [part for row in rows for part in split3(to_tiles(row))]
    moved = mxu(jnp.concatenate(parts, axis=0), at_lane)
    for k in range(len(rows)):
        three = [moved[(3 * k + s) * tiles:(3 * k + s + 1) * tiles] for s in range(3)]
        picked = jnp.where(at_tile, (three[0] + three[1]) + three[2], 0.0)
        fields_ref[k] = to_clusters(jnp.sum(picked, axis=0, keepdims=True), cluster)


def from_order(fields, perm_row, out_ref):
    tiles = perm_row.shape[1] // LANES
    at_tile, at_lane = place(perm_row, tiles)
    parts = []
    for field in fields:
        row = to_row_of_clusters(field)
        parts += [jnp.where(at_tile, part.astype(f32), 0.0).astype(bf16) for part in split3(row)]
    moved = mxu_nt(jnp.concatenate(parts, axis=0), at_lane)
    for k in range(len(fields)):
        three = [moved[(3 * k + s) * tiles:(3 * k + s + 1) * tiles] for s in range(3)]
        out_ref[k:k + 1, :] = to_row((three[0] + three[1]) + three[2])


def to_row_of_clusters(x):
    return jnp.concatenate([x[k:k + 1, :] for k in range(x.shape[0])], axis=1)


def one_hot(mask):
    return jnp.where(mask, 1.0, 0.0).astype(bf16)


def collect(mask, terms):
    hot = one_hot(mask)
    high = terms.astype(bf16)
    return mxu(hot, high) + mxu(hot, (terms - high.astype(f32)).astype(bf16))


def picked(at, values):
    hot = one_hot(lax.broadcasted_iota(jnp.int32, (at.shape[0], values.shape[0]), 1) == at)
    return mxu(hot, values).astype(bf16)


def pair_terms(at, ranks, values, product, given):
    x = picked(at, values)
    groups = at.shape[0] // PAIRS
    coefs = []
    for k in range(groups):
        rows = slice(k * PAIRS, (k + 1) * PAIRS)
        coef = product(x[rows], k)
        shape = coef.shape
        rank = lax.broadcasted_iota(jnp.int32, shape, 1) - shape[1] // PAIRS * lax.broadcasted_iota(jnp.int32, shape, 0)
        within = (rank >= 0) & (rank < ranks[rows])
        coefs.append(jnp.where(within, coef, 0.0).astype(bf16))
    return jnp.concatenate([mxu(coefs[k], given(k)) for k in range(groups)], axis=0)


def part_of(k, rows, head, tail):
    first = head.shape[0] // rows
    return head[pl.ds(k * rows, rows)] if k < first else tail[pl.ds((k - first) * rows, rows)]


def second_sums(chunk, everyone_ref, near_0_ref, near_1_ref, info_ref, col_ref, sources, heads, tails, sem, load_heads,
                kept_ref, sent_ref, right_t):
    pairs = info_ref.shape[1]
    rows = (heads[0].shape[0] + tails[0].shape[0]) // pairs * PAIRS
    fetched = []
    for which, (source, head, tail) in enumerate(zip(sources, heads, tails)):
        start = head.shape[0]
        copies = {}
        if load_heads:
            copies[0] = pltpu.make_async_copy(source.at[pl.ds(0, start)], head, sem.at[which, 0])
        for k in range(tail.shape[0] // chunk):
            part, at = pl.ds(k * chunk, chunk), start + k * chunk
            copies[at] = pltpu.make_async_copy(source.at[pl.ds(at, chunk)], tail.at[part], sem.at[which, k + 1])
        for copy in copies.values():
            copy.start()

        def group(k, head=head, tail=tail, copies=copies):
            if k * rows in copies:
                copies[k * rows].wait()
            return part_of(k, rows, head, tail)

        fetched.append(group)
    left_rows, right_rows = fetched

    def transposing(k):
        right = right_rows(k)
        right_t[:, pl.ds(k * rows, rows)] = jnp.transpose(right)
        return right

    terms = pair_terms(col_ref[:, 0:1], col_ref[:, 2:3], everyone_ref[...], lambda x, k: mxu_nt(x, left_rows(k)), transposing)
    halves(sums_at(info_ref, 1, 2 * kept_ref.shape[0], terms), kept_ref, sent_ref)
    half = near_0_ref.shape[0]
    kept_ref[0:half, :] += near_0_ref[...]
    kept_ref[half:2 * half, :] += near_1_ref[...]


def terms_to_second(chunk, everyone, near_0, near_1, info, col, left_hbm, right_hbm, kept, sent, left_head, right_head,
                    left, right_t, right, sem):
    second_sums(chunk, everyone, near_0, near_1, info, col, (left_hbm, right_hbm), (left_head, right_head), (left, right),
                sem, True, kept, sent, right_t)


def terms_to_second_again(chunk, everyone, near_0, near_1, info, col, left_head, right_head, left_hbm, right_hbm, kept, sent,
                          left, right_t, right, sem):
    second_sums(chunk, everyone, near_0, near_1, info, col, (left_hbm, right_hbm), (left_head, right_head), (left, right),
                sem, False, kept, sent, right_t)


def terms_to_first(line_ref, more_ref, info_ref, col_ref, left_head, left, right_t, first_ref):
    line = jnp.concatenate([line_ref[...], more_ref[...]], axis=0).astype(bf16)
    rows = right_t.shape[1] // info_ref.shape[1] * PAIRS
    terms = pair_terms(col_ref[:, 3:4], col_ref[:, 2:3], line, lambda x, k: mxu(x, right_t[:, pl.ds(k * rows, rows)]),
                       lambda k: part_of(k, rows, left_head, left))
    first_ref[...] = sums_at(info_ref, 0, first_ref.shape[0], terms)


def sums_at(info_ref, side, rows, terms):
    at = lax.broadcasted_iota(jnp.int32, (rows, info_ref.shape[1]), 0) == info_ref[side:side + 1, :]
    return collect(at, terms)


def halves(x, kept_ref, sent_ref):
    step = kept_ref.shape[0]
    kept_ref[...] = x[:step]
    sent_ref[...] = x[step:].astype(sent_ref.dtype)


def join(held_ref, received_ref, out_ref):
    out_ref[...] = jnp.concatenate([held_ref[...], received_ref[...]], axis=0)


def spread(own_ref, copies_ref):
    value = own_ref[...].astype(bf16)
    for k in range(copies_ref.shape[0]):
        copies_ref[k] = value


def add(held_ref, received_ref, *out_refs):
    halves(held_ref[...] + received_ref[...], *out_refs)


HOPS = (1, 3, 7)
BACK = (1, 7, 3)


def place_of(difference, hops):
    place = jnp.zeros_like(difference)
    for k in range(2 ** len(hops)):
        reached = 0
        for bit, hop in enumerate(hops):
            reached ^= hop * (k >> bit & 1)
        place = jnp.where(difference == reached, k, place)
    return place


def pair_info(own_count, columns, pairs_ref, ranks_ref, info_ref, col_ref):
    row = lax.axis_index("row")
    owner = lax.div(pairs_ref[...], own_count)
    inside = pairs_ref[...] - owner * own_count
    owner_row = lax.div(owner, columns)
    by_row = owner_row ^ row
    first_at = (owner - owner_row * columns) * own_count + inside
    second_at = place_of(by_row, HOPS) * own_count + inside
    second_sum_at = place_of(by_row, BACK) * own_count + inside
    count = ranks_ref.shape[1]
    sublane = lax.broadcasted_iota(jnp.int32, (count, LANES), 0)
    lane = lax.broadcasted_iota(jnp.int32, (count, LANES), 1)
    rank = jnp.sum(jnp.where(sublane == lane, jnp.broadcast_to(ranks_ref[...], (count, LANES)), 0), axis=1, keepdims=True)
    columns_of = jnp.where(lane == 0, first_at[:, 0:1], jnp.where(lane == 1, second_sum_at[:, 1:2], jnp.where(
        lane == 2, rank, second_at[:, 1:2])))
    col_ref[...] = columns_of
    info_ref[...] = jnp.transpose(columns_of)[:info_ref.shape[0]]


def near_terms(which, two_ref, near, out_ref):
    half = out_ref.shape[0]
    row_own = lax.broadcasted_iota(jnp.int32, out_ref.shape, 0)
    mine = two_ref[0:2 * half, :].astype(bf16)
    total = jnp.zeros(row_own.shape, f32)
    for k in range(half):
        product = mxu(mine, near[which * half + k])[which * half:(which + 1) * half]
        total += jnp.where(row_own == k, product, 0.0)
    out_ref[...] = total


def prepare(own_count, columns, _, pairs_ref, ranks_ref, state_ref, friction_ref, perm_ref, info_ref, col_ref, fields_ref):
    pair_info(own_count, columns, pairs_ref, ranks_ref, info_ref, col_ref)
    to_order(state_ref, friction_ref, perm_ref, fields_ref)


def slopes(lv, lt, a_sigma, b_sigma, stress):
    rate = jnp.exp(lv)
    dlt = jnp.exp(-lt) - rate
    return (stress - b_sigma * dlt) / (a_sigma + damping * rate), dlt


def total_stress(refs):
    from_first_ref, kept_ref, received_ref = refs
    parts = [from_first_ref[k] for k in range(from_first_ref.shape[0])]
    while len(parts) > 1:
        parts = [parts[k] + parts[k + 1] for k in range(0, len(parts), 2)]
    return parts[0] + (kept_ref[...] + received_ref[...])


def half_step(*refs):
    *stress_refs, fields_ref, slope_ref, own_ref = refs
    lv, lt, a_sigma, b_sigma = (fields_ref[k] for k in range(4))
    dlv, dlt = slopes(lv, lt, a_sigma, b_sigma, total_stress(stress_refs))
    slope_ref[0] = dlv
    slope_ref[1] = dlt
    own_ref[...] = (1.0 - jnp.exp(lv + step_size * dlv)).astype(bf16).astype(f32)


def last_step(*refs):
    *stress_refs, fields_ref, slope_ref, new_ref, sum_ref = refs
    lv, lt, a_sigma, b_sigma = (fields_ref[k] for k in range(4))
    first = (slope_ref[0], slope_ref[1])
    second = slopes(lv + step_size * first[0], lt + step_size * first[1], a_sigma, b_sigma, total_stress(stress_refs))
    squares = jnp.zeros(lv.shape, f32)
    for k, base in enumerate((lv, lt)):
        new = base + 0.5 * step_size * (first[k] + second[k])
        new_ref[k] = new
        scaled = 0.5 * step_size * (second[k] - first[k]) / (abs_tol + rel_tol * jnp.abs(new))
        squares += scaled * scaled
    sum_ref[...] = jnp.full(sum_ref.shape, jnp.sum(squares), f32)


def finish(entries, everywhere_ref, new_ref, perm_ref, out_ref, norm_ref):
    norm_ref[...] = jnp.sqrt(jnp.sum(everywhere_ref[...], axis=0, keepdims=True)[:, 0:1] / entries)
    from_order([new_ref[0], new_ref[1]], perm_ref[...], out_ref)


def in_hbm(x):
    return pltpu.with_memory_space_constraint(x, pltpu.HBM)


def call(kernel, out_shape, inputs, micros, scratch=(), streamed=()):
    many = isinstance(out_shape, (list, tuple))
    name = getattr(kernel, "func", kernel).__name__
    return pl.pallas_call(
        kernel,
        out_shape=out_shape,
        in_specs=[pl.BlockSpec(memory_space=pl.ANY) if any(x is y for y in streamed) else VMEM for x in inputs],
        out_specs=[VMEM] * len(out_shape) if many else VMEM,
        name=name,
        scratch_shapes=list(scratch),
        cost_estimate=pl.CostEstimate(flops=int(micros * 1.1e9), bytes_accessed=0, transcendentals=0),
        compiler_params=pltpu.CompilerParams(vmem_limit_bytes=32 * 1024 * 1024),
    )(*inputs)


def shards(rows, columns, state, friction, near_blocks, left_factor, right_factor, pairs, ranks, perm):
    own_count, cluster = near_blocks.shape[:2]
    count, width = left_factor.shape[:2]
    span = columns * own_count
    sds = jax.ShapeDtypeStruct
    block = sds((own_count, cluster), f32)
    perm_row = perm.reshape(1, -1)

    def swap(x, axis, distance):
        size = rows if axis == "row" else columns
        return lax.ppermute(x, axis, [(r, r ^ distance) for r in range(size)])

    own = call(first_deficit, block, [in_hbm(state), in_hbm(perm_row)], 6)
    near = near_blocks
    left = in_hbm(left_factor.reshape(count * width, cluster))
    right = in_hbm(right_factor.reshape(count * width, cluster))

    def block_of(blocks, dtype):
        return sds((blocks * own_count, cluster), dtype)

    chunk, head = 3072, HEAD
    tail = count * width - head
    scratch = [pltpu.VMEM((tail, cluster), bf16), pltpu.SemaphoreType.DMA((2, tail // chunk + 1))]
    kept_there = [pltpu.VMEM((head, cluster), bf16)] * 2
    loaded = [pltpu.VMEM((tail, cluster), bf16), pltpu.VMEM((cluster, count * width), bf16)]

    def exchange(own, prepared=None, heads=None):
        copies = call(spread, sds((columns, own_count, cluster), bf16), [own], 0.6)
        two = call(join, block_of(2, f32), [own, swap(own, "row", HOPS[0])], 0.1)
        if prepared is None:
            prepared = call(
                functools.partial(prepare, own_count, columns),
                [sds((8, count), jnp.int32), sds((count, LANES), jnp.int32), sds((4, own_count, cluster), f32)],
                [two, pairs, ranks.reshape(1, -1), state, friction, perm_row], 0.7)
        info, info_col, _ = prepared
        four = call(join, block_of(4, f32), [two, swap(two, "row", HOPS[1])], 0.1)
        more = swap(four, "row", HOPS[2])
        everyone = lax.all_to_all(copies, "col", 0, 0).reshape(span, cluster)
        near_term = [call(functools.partial(near_terms, k), sds((own_count // 2, cluster), f32), [two, near], 0.3)
                     for k in range(2)]
        if heads is None:
            kept, sent, *factors = call(
                functools.partial(terms_to_second, chunk), [block_of(4, f32)] * 2 + kept_there + loaded,
                [everyone, *near_term, info, info_col, left, right], 5, scratch, (left, right))
            heads, factors = factors[:2], factors[2:]
        else:
            kept, sent, *factors = call(
                functools.partial(terms_to_second_again, chunk), [block_of(4, f32)] * 2 + loaded,
                [everyone, *near_term, info, info_col, *heads, left, right], 5, scratch, (left, right))
        first = call(terms_to_first, block_of(columns, f32), [four, more, info, info_col, heads[0], *factors], 2.5)
        for blocks, hop, cost in ((2, BACK[2], 1.0), (1, BACK[1], 0.1)):
            kept, sent = call(add, [block_of(blocks, f32)] * 2, [kept, swap(sent, "row", hop)], cost)
        from_first = lax.all_to_all(first.reshape(columns, own_count, cluster), "col", 0, 0)
        return [from_first, kept, swap(sent, "row", BACK[0])], prepared, heads

    received, prepared, heads = exchange(own)
    fields = prepared[2]
    slope, own = call(half_step, [sds((2, own_count, cluster), f32), block], [*received, fields], 0.1)
    received, _, _ = exchange(own, prepared, heads)
    devices = rows * columns
    new, squares = call(last_step, [sds((2, own_count, cluster), f32), sds((devices, LANES), f32)],
                        [*received, fields, slope], 0.2)
    everywhere = lax.all_to_all(squares, ("row", "col"), 0, 0, tiled=True)
    entries = 2.0 * state.shape[1] * devices
    new_state, norm = call(functools.partial(finish, entries), [sds(state.shape, f32), sds((1, 1), f32)],
                           [everywhere, new, perm_row], 1)
    return new_state, norm.reshape(())


def solution(mesh):
    both = ("row", "col")
    placed = (P(None, both), P(None, both), P(both, None, None), P(both, None, None), P(both, None, None),
              P(both, None), P(both), P(both))
    return jax.shard_map(
        functools.partial(shards, mesh.shape["row"], mesh.shape["col"]),
        mesh=mesh,
        in_specs=placed,
        out_specs=(P(None, both), P()),
        check_vma=False,
    )
```

```python
import functools

import jax
import jax.numpy as jnp
from jax import lax
from jax.experimental import pallas as pl
from jax.experimental.pallas import tpu as pltpu
from jax.sharding import PartitionSpec as P

step_size = 0.1
damping = 0.5
abs_tol = 0.001
rel_tol = 0.001

f32 = jnp.float32
bf16 = jnp.bfloat16
LANES = 128
PAIRS = 16
HEAD = 2048
VMEM = pl.BlockSpec(memory_space=pltpu.VMEM)


def mxu(a, b):
    return lax.dot_general(a, b, (((1,), (0,)), ((), ())), preferred_element_type=f32)


def mxu_nt(a, b):
    return lax.dot_general(a, b, (((1,), (1,)), ((), ())), preferred_element_type=f32)


def to_tiles(row):
    return jnp.concatenate([row[:, k * LANES:(k + 1) * LANES] for k in range(row.shape[1] // LANES)], axis=0)


def to_row(tiles):
    return jnp.concatenate([tiles[k:k + 1, :] for k in range(tiles.shape[0])], axis=1)


def to_clusters(row, cluster):
    return jnp.concatenate([row[:, k * cluster:(k + 1) * cluster] for k in range(row.shape[1] // cluster)], axis=0)


def split3(x):
    hi = x.astype(bf16)
    rest = x - hi.astype(f32)
    mid = rest.astype(bf16)
    low = (rest - mid.astype(f32)).astype(bf16)
    return hi, mid, low


def place(perm_row, tiles):
    count = perm_row.shape[1]
    local = lax.rem(perm_row, count)
    tile = lax.div(local, LANES)
    lane = local - tile * LANES
    at_tile = lax.broadcasted_iota(jnp.int32, (tiles, count), 0) == tile
    at_lane = lax.broadcasted_iota(jnp.int32, (LANES, count), 0) == lane
    return at_tile, jnp.where(at_lane, 1.0, 0.0).astype(bf16)


def first_deficit(state_ref, perm_ref, own_ref):
    cluster = own_ref.shape[1]
    at_tile, at_lane = place(perm_ref[...], perm_ref.shape[1] // LANES)
    deficit = to_tiles(1.0 - jnp.exp(state_ref[0:1, :])).astype(bf16)
    picked = jnp.where(at_tile, mxu(deficit, at_lane), 0.0)
    own_ref[...] = to_clusters(jnp.sum(picked, axis=0, keepdims=True), cluster)


def to_order(state_ref, friction_ref, perm_ref, fields_ref):
    cluster = fields_ref.shape[2]
    tiles = perm_ref.shape[1] // LANES
    at_tile, at_lane = place(perm_ref[...], tiles)
    coef_a, coef_b, sigma = (friction_ref[k:k + 1, :] for k in range(3))
    rows = (state_ref[0:1, :], state_ref[1:2, :], coef_a * sigma, coef_b * sigma)
    parts = [part for row in rows for part in split3(to_tiles(row))]
    moved = mxu(jnp.concatenate(parts, axis=0), at_lane)
    for k in range(len(rows)):
        three = [moved[(3 * k + s) * tiles:(3 * k + s + 1) * tiles] for s in range(3)]
        picked = jnp.where(at_tile, (three[0] + three[1]) + three[2], 0.0)
        fields_ref[k] = to_clusters(jnp.sum(picked, axis=0, keepdims=True), cluster)


def from_order(fields, perm_row, out_ref):
    tiles = perm_row.shape[1] // LANES
    at_tile, at_lane = place(perm_row, tiles)
    parts = []
    for field in fields:
        row = to_row_of_clusters(field)
        parts += [jnp.where(at_tile, part.astype(f32), 0.0).astype(bf16) for part in split3(row)]
    moved = mxu_nt(jnp.concatenate(parts, axis=0), at_lane)
    for k in range(len(fields)):
        three = [moved[(3 * k + s) * tiles:(3 * k + s + 1) * tiles] for s in range(3)]
        out_ref[k:k + 1, :] = to_row((three[0] + three[1]) + three[2])


def to_row_of_clusters(x):
    return jnp.concatenate([x[k:k + 1, :] for k in range(x.shape[0])], axis=1)


def one_hot(mask):
    return jnp.where(mask, 1.0, 0.0).astype(bf16)


def collect(mask, terms):
    hot = one_hot(mask)
    high = terms.astype(bf16)
    return mxu(hot, high) + mxu(hot, (terms - high.astype(f32)).astype(bf16))


def picked(at, values):
    hot = one_hot(lax.broadcasted_iota(jnp.int32, (at.shape[0], values.shape[0]), 1) == at)
    return mxu(hot, values).astype(bf16)


def pair_terms(at, ranks, values, product, given):
    x = picked(at, values)
    groups = at.shape[0] // PAIRS
    coefs = []
    for k in range(groups):
        rows = slice(k * PAIRS, (k + 1) * PAIRS)
        coef = product(x[rows], k)
        shape = coef.shape
        rank = lax.broadcasted_iota(jnp.int32, shape, 1) - shape[1] // PAIRS * lax.broadcasted_iota(jnp.int32, shape, 0)
        within = (rank >= 0) & (rank < ranks[rows])
        coefs.append(jnp.where(within, coef, 0.0).astype(bf16))
    return jnp.concatenate([mxu(coefs[k], given(k)) for k in range(groups)], axis=0)


def part_of(k, rows, head, tail):
    first = head.shape[0] // rows
    return head[pl.ds(k * rows, rows)] if k < first else tail[pl.ds((k - first) * rows, rows)]


def second_sums(chunk, everyone_ref, near_0_ref, near_1_ref, info_ref, col_ref, sources, heads, tails, sem, load_heads,
                kept_ref, sent_ref, right_t):
    pairs = info_ref.shape[1]
    rows = (heads[0].shape[0] + tails[0].shape[0]) // pairs * PAIRS
    fetched = []
    for which, (source, head, tail) in enumerate(zip(sources, heads, tails)):
        start = head.shape[0]
        copies = {}
        if load_heads:
            copies[0] = pltpu.make_async_copy(source.at[pl.ds(0, start)], head, sem.at[which, 0])
        for k in range(tail.shape[0] // chunk):
            part, at = pl.ds(k * chunk, chunk), start + k * chunk
            copies[at] = pltpu.make_async_copy(source.at[pl.ds(at, chunk)], tail.at[part], sem.at[which, k + 1])
        for copy in copies.values():
            copy.start()

        def group(k, head=head, tail=tail, copies=copies):
            if k * rows in copies:
                copies[k * rows].wait()
            return part_of(k, rows, head, tail)

        fetched.append(group)
    left_rows, right_rows = fetched

    def transposing(k):
        right = right_rows(k)
        right_t[:, pl.ds(k * rows, rows)] = jnp.transpose(right)
        return right

    terms = pair_terms(col_ref[:, 0:1], col_ref[:, 2:3], everyone_ref[...], lambda x, k: mxu_nt(x, left_rows(k)), transposing)
    halves(sums_at(info_ref, 1, 2 * kept_ref.shape[0], terms), kept_ref, sent_ref)
    half = near_0_ref.shape[0]
    kept_ref[0:half, :] += near_0_ref[...]
    kept_ref[half:2 * half, :] += near_1_ref[...]


def terms_to_second(chunk, everyone, near_0, near_1, info, col, left_hbm, right_hbm, kept, sent, left_head, right_head,
                    left, right_t, right, sem):
    second_sums(chunk, everyone, near_0, near_1, info, col, (left_hbm, right_hbm), (left_head, right_head), (left, right),
                sem, True, kept, sent, right_t)


def terms_to_second_again(chunk, everyone, near_0, near_1, info, col, left_head, right_head, left_hbm, right_hbm, kept, sent,
                          left, right_t, right, sem):
    second_sums(chunk, everyone, near_0, near_1, info, col, (left_hbm, right_hbm), (left_head, right_head), (left, right),
                sem, False, kept, sent, right_t)


def terms_to_first(line_ref, more_ref, info_ref, col_ref, left_head, left, right_t, first_ref):
    line = jnp.concatenate([line_ref[...], more_ref[...]], axis=0).astype(bf16)
    rows = right_t.shape[1] // info_ref.shape[1] * PAIRS
    terms = pair_terms(col_ref[:, 1:2], col_ref[:, 2:3], line, lambda x, k: mxu(x, right_t[:, pl.ds(k * rows, rows)]),
                       lambda k: part_of(k, rows, left_head, left))
    first_ref[...] = sums_at(info_ref, 0, first_ref.shape[0], terms)


def sums_at(info_ref, side, rows, terms):
    at = lax.broadcasted_iota(jnp.int32, (rows, info_ref.shape[1]), 0) == info_ref[side:side + 1, :]
    return collect(at, terms)


def halves(x, kept_ref, sent_ref):
    step = kept_ref.shape[0]
    kept_ref[...] = x[:step]
    sent_ref[...] = x[step:].astype(sent_ref.dtype)


def join(held_ref, received_ref, out_ref):
    out_ref[...] = jnp.concatenate([held_ref[...], received_ref[...]], axis=0)


def spread(own_ref, copies_ref):
    value = own_ref[...].astype(bf16)
    for k in range(copies_ref.shape[0]):
        copies_ref[k] = value


def add(held_ref, received_ref, *out_refs):
    halves(held_ref[...] + received_ref[...], *out_refs)


HOPS = (1, 3, 7)


def place_of(difference):
    place = jnp.zeros_like(difference)
    for k in range(2 ** len(HOPS)):
        reached = 0
        for bit, hop in enumerate(HOPS):
            reached ^= hop * (k >> bit & 1)
        place = jnp.where(difference == reached, k, place)
    return place


def pair_info(own_count, columns, pairs_ref, ranks_ref, info_ref, col_ref):
    row = lax.axis_index("row")
    owner = lax.div(pairs_ref[...], own_count)
    inside = pairs_ref[...] - owner * own_count
    owner_row = lax.div(owner, columns)
    by_row = owner_row ^ row
    first_at = (owner - owner_row * columns) * own_count + inside
    second_at = place_of(by_row) * own_count + inside
    count = ranks_ref.shape[1]
    sublane = lax.broadcasted_iota(jnp.int32, (count, LANES), 0)
    lane = lax.broadcasted_iota(jnp.int32, (count, LANES), 1)
    rank = jnp.sum(jnp.where(sublane == lane, jnp.broadcast_to(ranks_ref[...], (count, LANES)), 0), axis=1, keepdims=True)
    columns_of = jnp.where(lane == 0, first_at[:, 0:1], jnp.where(lane == 1, second_at[:, 1:2], rank))
    col_ref[...] = columns_of
    info_ref[...] = jnp.transpose(columns_of)[:info_ref.shape[0]]


def near_terms(which, two_ref, near, out_ref):
    half = out_ref.shape[0]
    row_own = lax.broadcasted_iota(jnp.int32, out_ref.shape, 0)
    mine = two_ref[0:2 * half, :].astype(bf16)
    total = jnp.zeros(row_own.shape, f32)
    for k in range(half):
        product = mxu(mine, near[which * half + k])[which * half:(which + 1) * half]
        total += jnp.where(row_own == k, product, 0.0)
    out_ref[...] = total


def prepare(own_count, columns, _, pairs_ref, ranks_ref, state_ref, friction_ref, perm_ref, info_ref, col_ref, fields_ref):
    pair_info(own_count, columns, pairs_ref, ranks_ref, info_ref, col_ref)
    to_order(state_ref, friction_ref, perm_ref, fields_ref)


def slopes(lv, lt, a_sigma, b_sigma, stress):
    rate = jnp.exp(lv)
    dlt = jnp.exp(-lt) - rate
    return (stress - b_sigma * dlt) / (a_sigma + damping * rate), dlt


def total_stress(refs):
    from_first_ref, kept_ref, received_ref = refs
    parts = [from_first_ref[k] for k in range(from_first_ref.shape[0])]
    while len(parts) > 1:
        parts = [parts[k] + parts[k + 1] for k in range(0, len(parts), 2)]
    return parts[0] + (kept_ref[...] + received_ref[...])


def half_step(*refs):
    *stress_refs, fields_ref, slope_ref, own_ref = refs
    lv, lt, a_sigma, b_sigma = (fields_ref[k] for k in range(4))
    dlv, dlt = slopes(lv, lt, a_sigma, b_sigma, total_stress(stress_refs))
    slope_ref[0] = dlv
    slope_ref[1] = dlt
    own_ref[...] = (1.0 - jnp.exp(lv + step_size * dlv)).astype(bf16).astype(f32)


def last_step(*refs):
    *stress_refs, fields_ref, slope_ref, new_ref, sum_ref = refs
    lv, lt, a_sigma, b_sigma = (fields_ref[k] for k in range(4))
    first = (slope_ref[0], slope_ref[1])
    second = slopes(lv + step_size * first[0], lt + step_size * first[1], a_sigma, b_sigma, total_stress(stress_refs))
    squares = jnp.zeros(lv.shape, f32)
    for k, base in enumerate((lv, lt)):
        new = base + 0.5 * step_size * (first[k] + second[k])
        new_ref[k] = new
        scaled = 0.5 * step_size * (second[k] - first[k]) / (abs_tol + rel_tol * jnp.abs(new))
        squares += scaled * scaled
    sum_ref[...] = jnp.full(sum_ref.shape, jnp.sum(squares), f32)


def finish(entries, everywhere_ref, new_ref, perm_ref, out_ref, norm_ref):
    norm_ref[...] = jnp.sqrt(jnp.sum(everywhere_ref[...], axis=0, keepdims=True)[:, 0:1] / entries)
    from_order([new_ref[0], new_ref[1]], perm_ref[...], out_ref)


def in_hbm(x):
    return pltpu.with_memory_space_constraint(x, pltpu.HBM)


def call(kernel, out_shape, inputs, micros, scratch=(), streamed=()):
    many = isinstance(out_shape, (list, tuple))
    name = getattr(kernel, "func", kernel).__name__
    return pl.pallas_call(
        kernel,
        out_shape=out_shape,
        in_specs=[pl.BlockSpec(memory_space=pl.ANY) if any(x is y for y in streamed) else VMEM for x in inputs],
        out_specs=[VMEM] * len(out_shape) if many else VMEM,
        name=name,
        scratch_shapes=list(scratch),
        cost_estimate=pl.CostEstimate(flops=int(micros * 1.1e9), bytes_accessed=0, transcendentals=0),
        compiler_params=pltpu.CompilerParams(vmem_limit_bytes=32 * 1024 * 1024),
    )(*inputs)


def shards(rows, columns, state, friction, near_blocks, left_factor, right_factor, pairs, ranks, perm):
    own_count, cluster = near_blocks.shape[:2]
    count, width = left_factor.shape[:2]
    span = columns * own_count
    sds = jax.ShapeDtypeStruct
    block = sds((own_count, cluster), f32)
    perm_row = perm.reshape(1, -1)

    def swap(x, axis, distance):
        size = rows if axis == "row" else columns
        return lax.ppermute(x, axis, [(r, r ^ distance) for r in range(size)])

    own = call(first_deficit, block, [in_hbm(state), in_hbm(perm_row)], 6)
    near = near_blocks
    left = in_hbm(left_factor.reshape(count * width, cluster))
    right = in_hbm(right_factor.reshape(count * width, cluster))

    def block_of(blocks, dtype):
        return sds((blocks * own_count, cluster), dtype)

    chunk, head = 3072, HEAD
    tail = count * width - head
    scratch = [pltpu.VMEM((tail, cluster), bf16), pltpu.SemaphoreType.DMA((2, tail // chunk + 1))]
    kept_there = [pltpu.VMEM((head, cluster), bf16)] * 2
    loaded = [pltpu.VMEM((tail, cluster), bf16), pltpu.VMEM((cluster, count * width), bf16)]

    def exchange(own, prepared=None, heads=None):
        copies = call(spread, sds((columns, own_count, cluster), bf16), [own], 0.6)
        two = call(join, block_of(2, f32), [own, swap(own, "row", HOPS[0])], 0.1)
        if prepared is None:
            prepared = call(
                functools.partial(prepare, own_count, columns),
                [sds((8, count), jnp.int32), sds((count, LANES), jnp.int32), sds((4, own_count, cluster), f32)],
                [two, pairs, ranks.reshape(1, -1), state, friction, perm_row], 0.7)
        info, info_col, _ = prepared
        four = call(join, block_of(4, f32), [two, swap(two, "row", HOPS[1])], 0.1)
        more = swap(four, "row", HOPS[2])
        everyone = lax.all_to_all(copies, "col", 0, 0).reshape(span, cluster)
        near_term = [call(functools.partial(near_terms, k), sds((own_count // 2, cluster), f32), [two, near], 0.3)
                     for k in range(2)]
        if heads is None:
            kept, sent, *factors = call(
                functools.partial(terms_to_second, chunk), [block_of(4, f32)] * 2 + kept_there + loaded,
                [everyone, *near_term, info, info_col, left, right], 5, scratch, (left, right))
            heads, factors = factors[:2], factors[2:]
        else:
            kept, sent, *factors = call(
                functools.partial(terms_to_second_again, chunk), [block_of(4, f32)] * 2 + loaded,
                [everyone, *near_term, info, info_col, *heads, left, right], 5, scratch, (left, right))
        first = call(terms_to_first, block_of(columns, f32), [four, more, info, info_col, heads[0], *factors], 2.5)
        for blocks, hop, cost in ((2, HOPS[2], 1.0), (1, HOPS[1], 0.1)):
            kept, sent = call(add, [block_of(blocks, f32)] * 2, [kept, swap(sent, "row", hop)], cost)
        from_first = lax.all_to_all(first.reshape(columns, own_count, cluster), "col", 0, 0)
        return [from_first, kept, swap(sent, "row", HOPS[0])], prepared, heads

    received, prepared, heads = exchange(own)
    fields = prepared[2]
    slope, own = call(half_step, [sds((2, own_count, cluster), f32), block], [*received, fields], 0.1)
    received, _, _ = exchange(own, prepared, heads)
    devices = rows * columns
    new, squares = call(last_step, [sds((2, own_count, cluster), f32), sds((devices, LANES), f32)],
                        [*received, fields, slope], 0.2)
    everywhere = lax.all_to_all(squares, ("row", "col"), 0, 0, tiled=True)
    entries = 2.0 * state.shape[1] * devices
    new_state, norm = call(functools.partial(finish, entries), [sds(state.shape, f32), sds((1, 1), f32)],
                           [everywhere, new, perm_row], 1)
    return new_state, norm.reshape(())


def solution(mesh):
    both = ("row", "col")
    placed = (P(None, both), P(None, both), P(both, None, None), P(both, None, None), P(both, None, None),
              P(both, None), P(both), P(both))
    return jax.shard_map(
        functools.partial(shards, mesh.shape["row"], mesh.shape["col"]),
        mesh=mesh,
        in_specs=placed,
        out_specs=(P(None, both), P()),
        check_vma=False,
    )
```
